1024 devices in a mesh: sub: 128 (over y, z, core), grp: 8 (over x).
Axes of the slice: x: 8, y: 8, z: 8, core: 2. Of those that a mesh axis runs over, the one named last changes fastest.
Arguments:
- jump_rhs: float32 [8, 128, 8, 8, 128], P('grp', 'sub'), may hold values from -18 to 18
- schur_blocks: bfloat16 [8, 128, 8, 4, 128, 128], P('grp', 'sub'), as said below
- dirichlet_blocks: bfloat16 [8, 128, 8, 4, 128, 128], P('grp', 'sub'), as said below
- block_columns: int32 [8, 128, 8, 4], P('grp', 'sub'), may hold values from 0 to 7, as said below
- face_partner_slots: int32 [8, 128, 4], P('grp', 'sub'), may hold values from 0 to 3, each once within a row
- corner_basis: float32 [3, 8, 128, 8, 128], P(None, 'grp', 'sub'), may hold values from -0.5 to 0.5
- corner_owner: int32 [8, 128, 8], P('grp', 'sub'), may hold values from 0 to 1023
- coarse_inverse: float32 [8, 384, 384], P('grp'), as said below
Outputs:
- dual: float32 [8, 128, 8, 8, 128], P('grp', 'sub')
- residual: float32 [8, 128, 8, 8, 128], P('grp', 'sub')
The draws below stay inside these ranges and needn't reach their ends.
Inputs may be any that keep to these rules, and one draw needn't show every extreme that they name: `block_columns`: each block row holds 4 different block indices, the first being the row's own block; the pattern is symmetric: if row b of a subdomain stores column c, row c stores column b. `schur_blocks`: each subdomain's operator is symmetric: the block of row b at column c is the transpose of the block of row c at column b. `dirichlet_blocks`: each subdomain's operator is symmetric: the block of row b at column c is the transpose of the block of row c at column b. `coarse_inverse`: each owner's matrix is symmetric positive definite. `face_partner_slots`: each strip's row is a permutation of its 4 slots.
All inputs are finite; a program needn't handle non-finite values.
Results may differ from the reference program's by a relative error of at most 0.02.
Values sent between devices are 32-bit elements; how exact they have to be, the bound alone decides.
A program may use at most 32 MiB of HBM per device.

```python
import math
import jax
import jax.numpy as jnp
import numpy as np
from jax import lax

BW = 128
NB = 8
KB = 4
LC = 8
CPO = 128
ITERS = 2
SUB_DEV = 1
NG = 8
SR = 128
NSL = 4
NCORN = 1024
N_SUB = 128


def pattern_offsets():
    offsets = [0, NB // 2]
    mirror = [0, 1]
    for step in range(1, (KB - 2) // 2 + 1):
        offsets = offsets + [step, NB - step]
        mirror = mirror + [len(offsets) - 1, len(offsets) - 2]
    return (np.array(offsets, dtype=np.int32), np.array(mirror, dtype=np.int32))


def block_pattern(key):
    key = jax.random.fold_in(key, 13)
    offsets, mirror = pattern_offsets()
    scores = jax.random.randint(key, (NG, SR, NB), 0, 1 << 20) * NB + jnp.arange(NB, dtype=jnp.int32)
    order = jnp.argsort(scores, axis=-1).astype(jnp.int32)
    position = jnp.argsort(order, axis=-1).astype(jnp.int32)
    places = (position[..., None] + jnp.asarray(offsets)[None, None, None, :]) % NB
    columns = jnp.take_along_axis(order, places.reshape(NG, SR, NB * KB), axis=-1)
    return columns.reshape(NG, SR, NB, KB).astype(jnp.int32)


def symmetric_operator(base_key, constant, spread_values):
    columns = block_pattern(base_key)
    key = jax.random.fold_in(base_key, constant)
    offsets, mirror = pattern_offsets()
    shape = (NG, SR, NB, KB, BW, BW)
    noise = jax.random.normal(key, shape, jnp.float32)
    mirror_slots = jnp.asarray(mirror)

    def one_subdomain(source, indices):
        return source[indices, mirror_slots[None, :]]
    reflected = jax.vmap(jax.vmap(one_subdomain))(noise, columns)
    blended = noise + jnp.swapaxes(reflected, -1, -2)
    leading = (jnp.arange(KB) == 0).astype(jnp.float32)[:, None, None]
    identity = jnp.eye(BW, dtype=jnp.float32)
    return (leading * identity + blended * (spread_values / math.sqrt(2.0 * BW))).astype(jnp.bfloat16)


def rising_scale(low_scale, high_scale):
    strips = SR // SUB_DEV
    strip_index = (jnp.arange(SR, dtype=jnp.int32) // SUB_DEV).astype(jnp.float32)
    group_index = jnp.arange(NG, dtype=jnp.int32).astype(jnp.float32)
    place = (strip_index[None, :] * NG + group_index[:, None]) / max(strips * NG - 1, 1)
    ratio = math.log(high_scale / low_scale)
    return low_scale * jnp.exp(ratio * place)


def draw_jump_rhs(key, part):
    key = jax.random.fold_in(key, 19)
    shape = (NG, SR, NB, LC, BW)
    noise = jnp.clip(jax.random.normal(key, shape, jnp.float32), -6.0, 6.0)
    scales = rising_scale(0.5, 3.0)
    return noise * scales[:, :, None, None, None]


def draw_schur_blocks(key, part):
    return symmetric_operator(key, 11, 0.2)


def draw_dirichlet_blocks(key, part):
    return symmetric_operator(key, 12, 0.2)


def draw_block_columns(key, part):
    return block_pattern(key)


def draw_coarse_inverse(key, part):
    key = jax.random.fold_in(key, 17)
    order = 3 * CPO
    shape = (NG, order, order)
    noise = jax.random.normal(key, shape, jnp.float32)
    symmetric = (noise + jnp.swapaxes(noise, 1, 2)) * (0.25 / math.sqrt(order))
    return jnp.eye(order, dtype=jnp.float32) + symmetric


def plant(values, own_key, least, largest):
    extent = values.shape
    spot = [jax.random.randint(jax.random.fold_in(own_key, axis), (), 0, extent[axis]) for axis in range(len(extent))]
    values = values.at[tuple(spot)].set(least)
    longest = extent.index(max(extent))
    spot[longest] = (spot[longest] + 1) % extent[longest]
    return values.at[tuple(spot)].set(largest)


def steps_of(key, dims, cuts, low, largest):
    factor_of, own = 1.0, jax.random.fold_in(key, 6)
    for dim, shards_of in cuts:
        heights = jnp.exp(jax.random.uniform(jax.random.fold_in(own, dim), (shards_of,), jnp.float32, low / len(cuts), largest / len(cuts)))
        factor_of = factor_of * jnp.repeat(heights, dims[dim] // shards_of).reshape([-1 if axis == dim else 1 for axis in range(len(dims))])
    return factor_of


def centred(key, dims, scale, limit, shards=(), kind=jnp.bfloat16):
    gain = steps_of(key, dims, shards, -0.22, 0.18) if shards else 1.0
    result = jax.random.normal(key, dims, jnp.float32) * scale * gain
    return jnp.minimum(jnp.maximum(result, -limit), limit).astype(kind)


def setup_inputs(seed: int = 0) -> dict:
    splits = jax.random.split(jax.random.key(seed), 9)
    jump_rhs = draw_jump_rhs(jax.random.fold_in(splits[8], 71), 0)
    schur_blocks = draw_schur_blocks(jax.random.fold_in(splits[8], 71), 0)
    dirichlet_blocks = draw_dirichlet_blocks(jax.random.fold_in(splits[8], 71), 0)
    block_columns = draw_block_columns(jax.random.fold_in(splits[8], 71), 0)
    face_partner_slots = jax.vmap(lambda own: jax.random.permutation(own, NSL))(jax.random.split(splits[4], NG * N_SUB)).reshape((NG, N_SUB, NSL)).astype(jnp.int32)
    corner_basis = centred(splits[5], (3, NG, SR, NB, BW), BW ** -0.5, 0.5, ((1, 8), (2, 128)), jnp.float32)
    corner_owner = plant(jax.random.randint(splits[6], (NG, SR, NB), 0, NCORN), jax.random.fold_in(splits[6], 1), 0, NCORN - 1).astype(jnp.int32)
    coarse_inverse = draw_coarse_inverse(jax.random.fold_in(splits[8], 71), 0)
    return dict(jump_rhs=jump_rhs, schur_blocks=schur_blocks, dirichlet_blocks=dirichlet_blocks, block_columns=block_columns, face_partner_slots=face_partner_slots, corner_basis=corner_basis, corner_owner=corner_owner, coarse_inverse=coarse_inverse)


TOP_PRECISION = lax.Precision.HIGHEST


def partner(field, match):
    groups, strips, slot_count = match.shape
    per_strip = field.shape[1] // strips
    halfway = field.shape[2] // 2
    shaped = field.reshape(groups, strips, per_strip, field.shape[2], LC, BW)
    left_face = shaped[:, :, :, :halfway].reshape(groups, strips, slot_count, LC, BW)
    right_face = shaped[:, :, :, halfway:].reshape(groups, strips, slot_count, LC, BW)
    inverse = jnp.argsort(match, axis=-1).astype(jnp.int32)
    ordered = jnp.take_along_axis(left_face, inverse[:, :, :, None, None], axis=2)
    new_left = jnp.take_along_axis(jnp.roll(right_face, 1, axis=1), match[:, :, :, None, None], axis=2)
    new_right = jnp.roll(ordered, -1, axis=1)
    joined = jnp.concatenate([new_left.reshape(groups, strips, per_strip, halfway, LC, BW), new_right.reshape(groups, strips, per_strip, halfway, LC, BW)], axis=3)
    return joined.reshape(field.shape)


def block_product(matrices, columns, field):
    def per_group(operands):
        group_blocks, group_columns, grouped_values = operands
        lowered = grouped_values.astype(jnp.bfloat16).astype(jnp.float32)
        picked = jax.vmap(lambda source, indices: source[indices])(lowered, group_columns)
        return jnp.einsum("sbkij,sbklj->sbli", group_blocks.astype(jnp.float32), picked, precision=TOP_PRECISION)
    return lax.map(per_group, (matrices, columns, field))


def coarse_term(field, basis, owners, inverse):
    terms = jnp.einsum("cgsbi,gsbli->gsbcl", basis, field, precision=TOP_PRECISION)
    assembled = jax.ops.segment_sum(terms.reshape(-1, 3, LC), owners.reshape(-1), num_segments=NCORN)
    grouped = assembled.reshape(NG, CPO, 3, LC)
    solved = jnp.einsum("gaqbr,grbl->gqal", inverse.reshape(NG, 3, CPO, 3, CPO), grouped, precision=TOP_PRECISION)
    spread_values = solved.reshape(NCORN, 3, LC)[owners]
    return jnp.einsum("cgsbi,gsbcl->gsbli", basis, spread_values, precision=TOP_PRECISION)


def inner(first, second):
    return jnp.sum(first * second, axis=(0, 1, 2, 4))


def reference(jump_rhs, schur_blocks, dirichlet_blocks, block_columns, face_partner_slots, corner_basis, corner_owner, coarse_inverse):
    def jump(field):
        return field - partner(field, face_partner_slots)

    def flexibility(direction):
        spread_values = jump(direction)
        return jump(block_product(schur_blocks, block_columns, spread_values) + coarse_term(spread_values, corner_basis, corner_owner, coarse_inverse))

    def precondition(current):
        return jump(block_product(dirichlet_blocks, block_columns, jump(current)))

    residual = jump(jump_rhs)
    dual = jnp.zeros_like(residual)
    search = precondition(residual)
    direction = search
    product = inner(residual, search)
    for iteration in range(ITERS):
        image = flexibility(direction)
        alpha = product / inner(direction, image)
        dual = dual + alpha[:, None] * direction
        residual = residual - alpha[:, None] * image
        if iteration + 1 < ITERS:
            search = precondition(residual)
            renewed = inner(residual, search)
            direction = search + (renewed / product)[:, None] * direction
            product = renewed
    return dual, residual
```

```python
import functools

import jax
import jax.numpy as jnp
from jax import lax
from jax.experimental import pallas as pl
from jax.experimental.pallas import tpu as pltpu
from jax.sharding import PartitionSpec as P

MESH = pl.DeviceIdType.MESH
F32 = jnp.float32
BF16 = jnp.bfloat16
W = 128
LC = 8
NB = 8
HALF = 4
KB = 4
NJ = 16
LIVE = 3 * NJ
LANE_ENERGY = 48
LANE_SCAL = 50


def plan(sub_count, grp_count):
    chips = sub_count // 2
    along_z = 1
    while along_z * along_z < chips:
        along_z *= 2
    return chips // along_z, along_z, grp_count


def split(x):
    high = x.astype(BF16)
    low = (x - high.astype(F32)).astype(BF16)
    return high, low


def nn(a, b):
    return lax.dot_general(a, b, (((1,), (0,)), ((), ())), preferred_element_type=F32)


def nt(a, b):
    return lax.dot_general(a, b, (((1,), (1,)), ((), ())), preferred_element_type=F32)


def kernel(
    sizes,
    cols,
    match,
    owner,
    rhs_hbm,
    schur_hbm,
    dirichlet_hbm,
    basis_hbm,
    inverse_hbm,
    dual_out,
    residual_out,
    rhs,
    schur,
    dirichlet,
    basis,
    inverse,
    table,
    parts,
    faces,
    halo,
    nb_send,
    nb_recv,
    spread,
    own_send,
    own_recv,
    onehot,
    inv_split,
    a_send,
    a_recv,
    b_recv,
    c_recv,
    d_send,
    d_recv,
    fields,
    load_sem,
    halo_send_sem,
    halo_sem,
    nb_send_sem,
    nb_sem,
    own_send_sem,
    own_sem,
    a_send_sem,
    a_sem,
    b_send_sem,
    b_sem,
    c_send_sem,
    c_sem,
    d_send_sem,
    d_sem,
):
    ny, nz, nx = sizes
    strips = ny * nz * 2
    k = lax.axis_index("sub")
    g = lax.axis_index("grp")
    core = lax.rem(k, 2)
    zi = lax.rem(k // 2, nz)
    yi = k // (2 * nz)

    def dev(sub, grp):
        return {"sub": sub, "grp": grp}

    up = dev(lax.rem(k + 1, strips), g)
    down = dev(lax.rem(k + strips - 1, strips), g)

    def line_x(step, other):
        sub = (k + 1 - 2 * core) if other else k
        return dev(sub, lax.rem(g + step, nx))

    def line_y(step):
        return dev((lax.rem(yi + step, ny) * nz + zi) * 2 + core, g)

    def line_z(step):
        return dev((yi * nz + lax.rem(zi + step, nz)) * 2 + core, g)

    x_peers = [(t, o) for t in range(nx) for o in (0, 1) if (t, o) != (0, 0)]

    loads = []
    for n, (source, target) in enumerate(
        (
            (rhs_hbm, rhs),
            (basis_hbm, basis),
            (dirichlet_hbm, dirichlet),
            (inverse_hbm, inverse),
            (schur_hbm, schur),
        )
    ):
        copy = pltpu.make_async_copy(source, target, load_sem.at[n])
        copy.start()
        loads.append(copy)

    barrier = pltpu.get_barrier_semaphore()
    greeted = [up, down]
    greeted += [line_x(t, o) for t, o in x_peers]
    greeted += [line_y(t) for t in range(1, ny)]
    greeted += [line_z(t) for t in range(1, nz)]
    for peer in greeted:
        pl.semaphore_signal(barrier, inc=1, device_id=peer, device_id_type=MESH)

    at = [match[0, i] for i in range(HALF)]
    block_at = []
    for j in range(HALF):
        found = jnp.int32(0)
        for i in range(1, HALF):
            found = found + jnp.where(at[i] == j, jnp.int32(i), jnp.int32(0))
        block_at.append(found)
    block_at += [jnp.int32(b) for b in range(HALF, NB)]
    place_of = at + [jnp.int32(b) for b in range(HALF, NB)]

    for p in range(NB):
        b = block_at[p]
        table[p * KB] = b * KB
        for s in range(1, KB):
            c = cols[b, s]
            back = jnp.int32(0)
            for t in range(1, KB):
                back = back + jnp.where(cols[c, t] == b, jnp.int32(t), jnp.int32(0))
            table[p * KB + s] = c * KB + back

    loads[0].wait()
    for p in range(NB):
        faces[0, p] = rhs[block_at[p]]
    pl.semaphore_wait(barrier, len(greeted))

    def send_halo(stage):
        for side, peer in ((1, down), (0, up)):
            pltpu.make_async_remote_copy(
                src_ref=faces.at[stage, pl.ds(0 if side else HALF, HALF)],
                dst_ref=halo.at[stage, side],
                send_sem=halo_send_sem.at[stage],
                recv_sem=halo_sem.at[stage],
                device_id=peer,
                device_id_type=MESH,
            ).start()

    def whole(ref, send, recv):
        return pltpu.make_async_remote_copy(
            src_ref=ref, dst_ref=ref, send_sem=send, recv_sem=recv, device_id=up, device_id_type=MESH
        )

    def wait_halo(stage):
        whole(halo.at[stage], halo_send_sem.at[stage], halo_sem.at[stage]).wait_recv()

    def jump(stage):
        low = [faces[stage, p] - halo[stage, 0, p] for p in range(HALF)]
        high = [faces[stage, HALF + p] - halo[stage, 1, p] for p in range(HALF)]
        return low + high

    send_halo(0)

    lane = lax.broadcasted_iota(jnp.int32, (8, W), 1)
    lane_mode = lane // NJ
    lane_slot = lax.rem(lane, NJ)
    loads[1].wait()
    owners = [owner[0, block_at[p]].astype(F32) for p in range(NB)]
    for side in (0, 1):
        nb_send[side] = jnp.zeros((16, W), F32)
        for c in range(3):
            for j in range(HALF):
                p = j if side else HALF + j
                nb_send[side, c * HALF + j] = basis[c, block_at[p]]
        tag = jnp.zeros((8, W), F32)
        for j in range(HALF):
            p = j if side else HALF + j
            spot = NB + j + (HALF if side else 0)
            tag = jnp.where((lane_slot == spot) & (lane < LIVE), owners[p], tag)
        nb_send[side, 12] = tag[0]
    for side, peer in ((1, down), (0, up)):
        pltpu.make_async_remote_copy(
            src_ref=nb_send.at[side],
            dst_ref=nb_recv.at[side],
            send_sem=nb_send_sem,
            recv_sem=nb_sem,
            device_id=peer,
            device_id_type=MESH,
        ).start()

    def block_product(matrix, source):
        for b in range(NB):
            high, low = split(fields[source, place_of[b]])
            row = jnp.concatenate([high, low], axis=0)
            product = nn(row, jnp.concatenate([matrix[b, s] for s in range(KB)], axis=1))
            product = product[:LC] + product[LC:]
            for s in range(KB):
                parts[b * KB + s] = product[:, s * W : (s + 1) * W]
        result = []
        for p in range(NB):
            total = parts[table[p * KB]]
            for s in range(1, KB):
                total = total + parts[table[p * KB + s]]
            result.append(total)
        return result

    def inner(first, second):
        total = first[0] * second[0]
        for u, v in zip(first[1:], second[1:]):
            total = total + u * v
        return jnp.sum(total, axis=1, keepdims=True)

    wait_halo(0)
    residual = jump(0)
    for p in range(NB):
        fields[0, p] = residual[p] + residual[p]
    loads[2].wait()
    lifted = block_product(dirichlet, 0)
    for p in range(NB):
        faces[1, p] = lifted[p]
    send_halo(1)
    rz0 = inner([fields[0, p] for p in range(NB)], lifted)

    whole(nb_recv, nb_send_sem, nb_sem).wait_recv()
    own_lanes = nb_recv[0, pl.ds(12, 1)] + nb_recv[1, pl.ds(12, 1)]
    own_lanes = jnp.broadcast_to(own_lanes, (8, W))
    for p in range(NB):
        own_lanes = jnp.where((lane_slot == p) & (lane < LIVE), owners[p], own_lanes)
    own_lanes = jnp.where(lane < LIVE, own_lanes, -1.0)
    own_send[0] = own_lanes[:4]
    own_send[1] = pltpu.roll(own_lanes, 64, 1)[:4]
    own_recv[0] = own_lanes[:4]
    for t, o in x_peers:
        pltpu.make_async_remote_copy(
            src_ref=own_send.at[o],
            dst_ref=own_recv.at[2 * t + o],
            send_sem=own_send_sem,
            recv_sem=own_sem,
            device_id=line_x(t, o),
            device_id_type=MESH,
        ).start()

    rows = []
    for c in range(3):
        rows += [basis[c, pl.ds(block_at[p], 1)] for p in range(HALF)]
        rows.append(basis[c, HALF:NB])
        rows.append(-nb_recv[0, c * HALF : (c + 1) * HALF])
        rows.append(-nb_recv[1, c * HALF : (c + 1) * HALF])
    rows = jnp.concatenate(rows + [jnp.zeros((W - LIVE, W), F32)], axis=0)
    row_place = lax.rem(lax.broadcasted_iota(jnp.int32, (W, W), 0), NB)
    for p in range(NB):
        high, low = split(jnp.where(row_place == p, rows, 0.0))
        spread[0, :, p * W : (p + 1) * W] = high
        spread[1, :, p * W : (p + 1) * W] = low

    def send_corner_sums(turn, lifted):
        doubled = jnp.concatenate([u + u for u in lifted], axis=1)
        high, low = split(doubled)
        first = nt(jnp.concatenate([high, low], axis=0), spread[0])
        sums = first[:LC] + first[LC:] + nt(high, spread[1])
        rolled = pltpu.roll(sums, 64, 1)
        mine = jnp.where(core == 0, sums[:4], sums[4:])
        a_send[turn, 0] = mine
        a_send[turn, 1] = jnp.where(core == 0, rolled[4:], rolled[:4])
        a_recv[turn, 0] = mine
        for t, o in x_peers:
            pltpu.make_async_remote_copy(
                src_ref=a_send.at[turn, o],
                dst_ref=a_recv.at[turn, 2 * t + o],
                send_sem=a_send_sem.at[turn],
                recv_sem=a_sem.at[turn],
                device_id=line_x(t, o),
                device_id_type=MESH,
            ).start()

    def pair(ref):
        high = ref.astype(BF16).astype(F32)
        return jnp.concatenate([high, ref - high], axis=0).astype(BF16)

    def assemble(turn, scalars):
        whole(a_recv.at[turn, pl.ds(1, 2 * nx - 1)], a_send_sem.at[turn], a_sem.at[turn]).wait_recv()
        came = jnp.concatenate([a_recv[turn, 2 * t] + a_recv[turn, 2 * t + 1] for t in range(nx)], axis=1)
        dense = nt(pair(came), onehot[...])
        dense = dense[:4] + dense[4:]
        b_recv[turn, 0, 0] = jnp.concatenate([dense[:, :W], dense[:, W : 2 * W]], axis=0)
        b_recv[turn, 0, 1] = jnp.concatenate([dense[:, 2 * W :], scalars], axis=0)
        for t in range(1, ny):
            pltpu.make_async_remote_copy(
                src_ref=b_recv.at[turn, 0],
                dst_ref=b_recv.at[turn, t],
                send_sem=b_send_sem.at[turn],
                recv_sem=b_sem.at[turn],
                device_id=line_y(t),
                device_id_type=MESH,
            ).start()

    def total_of(ref, turn, count):
        sums = []
        for h in range(2):
            total = ref[turn, 0, h]
            for t in range(1, count):
                total = total + ref[turn, t, h]
            sums.append(total)
        return sums

    def across_z(turn):
        whole(b_recv.at[turn, pl.ds(1, ny - 1)], b_send_sem.at[turn], b_sem.at[turn]).wait_recv()
        for h, total in enumerate(total_of(b_recv, turn, ny)):
            c_recv[turn, 0, h] = total
        for t in range(1, nz):
            pltpu.make_async_remote_copy(
                src_ref=c_recv.at[turn, 0],
                dst_ref=c_recv.at[turn, t],
                send_sem=c_send_sem.at[turn],
                recv_sem=c_sem.at[turn],
                device_id=line_z(t),
                device_id_type=MESH,
            ).start()

    def solve(turn):
        whole(c_recv.at[turn, pl.ds(1, nz - 1)], c_send_sem.at[turn], c_sem.at[turn]).wait_recv()
        first, second = total_of(c_recv, turn, nz)
        summed = jnp.concatenate([first[:4], first[4:], second[:4]], axis=1)
        lhs = pair(summed)
        solved = nn(lhs, inv_split[0])
        solved = solved[:4] + solved[4:] + nn(lhs, inv_split[1])[:4]
        energy = jnp.sum(summed * solved, axis=1, keepdims=True)
        chosen = nn(pair(solved), onehot[...])
        chosen = chosen[:4] + chosen[4:]
        lane4 = lane[:4]
        extra = jnp.where(lane4 == LANE_ENERGY, energy, second[4:])
        aside = (lane4 >= LANE_ENERGY) & (lane4 < 64)
        for t in range(nx):
            d_send[turn, t] = jnp.where(aside, extra, chosen[:, t * W : (t + 1) * W])
        d_recv[turn, 0] = d_send[turn, 0]
        for t, o in x_peers:
            pltpu.make_async_remote_copy(
                src_ref=d_send.at[turn, t],
                dst_ref=d_recv.at[turn, 2 * t + o],
                send_sem=d_send_sem.at[turn],
                recv_sem=d_sem.at[turn],
                device_id=line_x(nx - t, o),
                device_id_type=MESH,
            ).start()

    def gathered(turn):
        whole(d_recv.at[turn, pl.ds(1, 2 * nx - 1)], d_send_sem.at[turn], d_sem.at[turn]).wait_recv()
        same, other = d_recv[turn, 0], d_recv[turn, 1]
        for t in range(1, nx):
            same = same + d_recv[turn, 2 * t]
            other = other + d_recv[turn, 2 * t + 1]
        both = jnp.where(
            core == 0, jnp.concatenate([same, other], axis=0), jnp.concatenate([other, same], axis=0)
        )
        turned = pltpu.roll(both, 64, 1)
        row_core = lax.broadcasted_iota(jnp.int32, (8, W), 0) // 4
        values = jnp.where(lane < LIVE, jnp.where(row_core == core, both, turned), 0.0)
        high, low = split(values)
        mixed = nn(jnp.concatenate([high, low], axis=0), spread[0])
        mixed = mixed[:LC] + mixed[LC:] + nn(high, spread[1])
        return [mixed[:, p * W : (p + 1) * W] for p in range(NB)], both, same + other

    send_corner_sums(0, lifted)

    whole(own_recv.at[pl.ds(1, 2 * nx - 1)], own_send_sem, own_sem).wait_recv()
    corner = lax.broadcasted_iota(jnp.int32, (W, W), 0).astype(F32)
    base = (g * W).astype(F32)
    lane1 = lane[:1]
    for t in range(nx):
        ids = jnp.where(lane1 < 64, own_recv[2 * t, pl.ds(0, 1)], own_recv[2 * t + 1, pl.ds(0, 1)]) - base
        for c in range(3):
            masked = jnp.where(lax.rem(lane1, 64) // NJ == c, ids, -1.0)
            onehot[c * W : (c + 1) * W, t * W : (t + 1) * W] = jnp.where(corner == masked, 1.0, 0.0).astype(BF16)

    assemble(0, jnp.zeros((4, W), F32))

    def apply_schur(stage, source):
        wait_halo(stage - 1)
        for p, value in enumerate(jump(stage - 1)):
            fields[source, p] = value + value
        product = block_product(schur, source)
        for p in range(NB):
            faces[stage, p] = product[p]
        send_halo(stage)
        return product

    loads[4].wait()
    apply_schur(2, 1)
    across_z(0)
    loads[3].wait()
    high, low = split(inverse[...])
    inv_split[0] = high
    inv_split[1] = low
    solve(0)
    mixed, _, _ = gathered(0)
    wait_halo(2)
    image = [u + v for u, v in zip(jump(2), mixed)]
    for p in range(NB):
        fields[2, p] = image[p] + image[p]

    lifted = block_product(dirichlet, 2)
    for p in range(NB):
        faces[3, p] = lifted[p]
    send_halo(3)
    send_corner_sums(1, lifted)
    doubled = [fields[2, p] for p in range(NB)]
    g1 = inner([fields[1, p] for p in range(NB)], doubled) * 0.25
    m1 = inner(doubled, lifted)
    product = apply_schur(4, 3)
    h1 = inner([fields[3, p] for p in range(NB)], product)
    lane_of = LANE_SCAL
    scalars = jnp.zeros((8, W), F32)
    row_half = lax.broadcasted_iota(jnp.int32, (8, W), 0) // 4
    for n, value in enumerate((rz0, g1, m1, h1)):
        scalars = jnp.where(lane == lane_of + n + 4 * row_half, value, scalars)
    assemble(1, scalars[:4] + scalars[4:])
    across_z(1)
    solve(1)
    mixed, both, sums = gathered(1)

    def pick(n):
        low = jnp.sum(jnp.where(lane[:4] == LANE_SCAL + n, sums, 0.0), axis=1, keepdims=True)
        high = jnp.sum(jnp.where(lane[:4] == LANE_SCAL + 4 + n, sums, 0.0), axis=1, keepdims=True)
        return jnp.concatenate([low, high], axis=0)

    rz0, g1, m1, h1 = (pick(n) for n in range(4))
    h1 = h1 + jnp.sum(jnp.where(lane == LANE_ENERGY, both, 0.0), axis=1, keepdims=True)
    alpha0 = rz0 / g1
    rz1 = alpha0 * alpha0 * m1 - rz0
    grow = 1.0 + rz1 / rz0
    energy = grow * grow * g1 - 2.0 * grow * alpha0 * m1 + alpha0 * alpha0 * h1
    alpha1 = rz1 / energy
    first = alpha0 + alpha1 * grow
    second = -alpha1 * alpha0
    wait_halo(4)
    last = [u + v for u, v in zip(jump(4), mixed)]
    for p in range(NB):
        parts[p] = 0.5 * (first * fields[1, p] + second * fields[3, p])
        parts[NB + p] = 0.5 * (fields[0, p] - first * fields[2, p]) - second * last[p]
    for b in range(NB):
        dual_out[b] = parts[place_of[b]]
        residual_out[b] = parts[place_of[b] + NB]

    for stage in range(5):
        whole(halo.at[stage], halo_send_sem.at[stage], halo_sem.at[stage]).wait_send()
    whole(nb_send, nb_send_sem, nb_sem).wait_send()
    whole(own_recv.at[pl.ds(1, 2 * nx - 1)], own_send_sem, own_sem).wait_send()
    for turn in (0, 1):
        whole(a_recv.at[turn, pl.ds(1, 2 * nx - 1)], a_send_sem.at[turn], a_sem.at[turn]).wait_send()
        whole(b_recv.at[turn, pl.ds(1, ny - 1)], b_send_sem.at[turn], b_sem.at[turn]).wait_send()
        whole(c_recv.at[turn, pl.ds(1, nz - 1)], c_send_sem.at[turn], c_sem.at[turn]).wait_send()
        whole(d_recv.at[turn, pl.ds(1, 2 * nx - 1)], d_send_sem.at[turn], d_sem.at[turn]).wait_send()


def shards(
    sizes,
    jump_rhs,
    schur_blocks,
    dirichlet_blocks,
    block_columns,
    face_partner_slots,
    corner_basis,
    corner_owner,
    coarse_inverse,
):
    ny, nz, nx = sizes
    field = jax.ShapeDtypeStruct((NB, LC, W), F32)
    smem = pl.BlockSpec(memory_space=pltpu.SMEM)
    far = pl.BlockSpec(memory_space=pl.ANY)
    near = pl.BlockSpec(memory_space=pltpu.VMEM)
    dma = pltpu.SemaphoreType.DMA
    dual, residual = pl.pallas_call(
        functools.partial(kernel, sizes),
        out_shape=(field, field),
        in_specs=[smem] * 3 + [far] * 5,
        out_specs=(near, near),
        scratch_shapes=[
            pltpu.VMEM((NB, LC, W), F32),
            pltpu.VMEM((NB, KB, W, W), BF16),
            pltpu.VMEM((NB, KB, W, W), BF16),
            pltpu.VMEM((3, NB, W), F32),
            pltpu.VMEM((3 * W, 3 * W), F32),
            pltpu.SMEM((NB * KB,), jnp.int32),
            pltpu.VMEM((NB * KB, LC, W), F32),
            pltpu.VMEM((5, NB, LC, W), F32),
            pltpu.VMEM((5, 2, HALF, LC, W), F32),
            pltpu.VMEM((2, 16, W), F32),
            pltpu.VMEM((2, 16, W), F32),
            pltpu.VMEM((2, W, NB * W), BF16),
            pltpu.VMEM((2, 4, W), F32),
            pltpu.VMEM((2 * nx, 4, W), F32),
            pltpu.VMEM((3 * W, nx * W), BF16),
            pltpu.VMEM((2, 3 * W, 3 * W), BF16),
            pltpu.VMEM((2, 2, 4, W), F32),
            pltpu.VMEM((2, 2 * nx, 4, W), F32),
            pltpu.VMEM((2, ny, 2, 8, W), F32),
            pltpu.VMEM((2, nz, 2, 8, W), F32),
            pltpu.VMEM((2, nx, 4, W), F32),
            pltpu.VMEM((2, 2 * nx, 4, W), F32),
            pltpu.VMEM((4, NB, LC, W), F32),
            dma((5,)),
            dma((5,)),
            dma((5,)),
            dma(()),
            dma(()),
            dma(()),
            dma(()),
            dma((2,)),
            dma((2,)),
            dma((2,)),
            dma((2,)),
            dma((2,)),
            dma((2,)),
            dma((2,)),
            dma((2,)),
        ],
        compiler_params=pltpu.CompilerParams(
            collective_id=0, has_side_effects=True, vmem_limit_bytes=32 * 1024 * 1024
        ),
    )(
        block_columns[0, 0],
        face_partner_slots[0],
        corner_owner[0],
        jump_rhs[0, 0],
        schur_blocks[0, 0],
        dirichlet_blocks[0, 0],
        corner_basis[:, 0, 0],
        coarse_inverse[0],
    )
    return dual[None, None], residual[None, None]


def solution(mesh):
    sizes = plan(mesh.shape["sub"], mesh.shape["grp"])
    placed = (
        P("grp", "sub", None, None, None),
        P("grp", "sub", None, None, None, None),
        P("grp", "sub", None, None, None, None),
        P("grp", "sub", None, None),
        P("grp", "sub", None),
        P(None, "grp", "sub", None, None),
        P("grp", "sub", None),
        P("grp", None, None),
    )
    return jax.shard_map(
        functools.partial(shards, sizes),
        mesh=mesh,
        in_specs=placed,
        out_specs=(P("grp", "sub", None, None, None), P("grp", "sub", None, None, None)),
        check_vma=False,
    )
```

```python
import functools

import jax
import jax.numpy as jnp
from jax import lax
from jax.experimental import pallas as pl
from jax.experimental.pallas import tpu as pltpu
from jax.sharding import PartitionSpec as P

MESH = pl.DeviceIdType.MESH
F32 = jnp.float32
BF16 = jnp.bfloat16
W = 128
LC = 8
NB = 8
HALF = 4
KB = 4
NJ = 16
LIVE = 3 * NJ
LANE_ENERGY = 48
LANE_SCAL = 50


def plan(sub_count, grp_count):
    chips = sub_count // 2
    along_z = 1
    while along_z * along_z < chips:
        along_z *= 2
    return chips // along_z, along_z, grp_count


def far_first(count):
    return sorted(range(1, count), key=lambda t: -min(t, count - t))


def split(x):
    high = x.astype(BF16)
    low = (x - high.astype(F32)).astype(BF16)
    return high, low


def nn(a, b):
    return lax.dot_general(a, b, (((1,), (0,)), ((), ())), preferred_element_type=F32)


def nt(a, b):
    return lax.dot_general(a, b, (((1,), (1,)), ((), ())), preferred_element_type=F32)


def kernel(
    sizes,
    cols_hbm,
    match_hbm,
    owner_hbm,
    rhs_hbm,
    schur_hbm,
    dirichlet_hbm,
    basis_hbm,
    inverse_hbm,
    dual_out,
    residual_out,
    cols,
    match,
    owner,
    rhs,
    schur,
    dirichlet,
    basis,
    inverse,
    table,
    parts,
    faces,
    halo,
    nb_send,
    nb_recv,
    spread,
    own_send,
    own_recv,
    onehot,
    inv_split,
    a_send,
    a_recv,
    b_recv,
    c_recv,
    d_send,
    d_recv,
    fields,
    load_sem,
    halo_send_sem,
    halo_sem,
    nb_send_sem,
    nb_sem,
    own_send_sem,
    own_sem,
    a_send_sem,
    a_sem,
    b_send_sem,
    b_sem,
    c_send_sem,
    c_sem,
    d_send_sem,
    d_sem,
):
    ny, nz, nx = sizes
    strips = ny * nz * 2
    k = lax.axis_index("sub")
    g = lax.axis_index("grp")
    core = lax.rem(k, 2)
    zi = lax.rem(k // 2, nz)
    yi = k // (2 * nz)

    def dev(sub, grp):
        return {"sub": sub, "grp": grp}

    up = dev(lax.rem(k + 1, strips), g)
    down = dev(lax.rem(k + strips - 1, strips), g)

    def line_x(step, other):
        sub = (k + 1 - 2 * core) if other else k
        return dev(sub, lax.rem(g + step, nx))

    def line_y(step):
        return dev((lax.rem(yi + step, ny) * nz + zi) * 2 + core, g)

    def line_z(step):
        return dev((yi * nz + lax.rem(zi + step, nz)) * 2 + core, g)

    x_peers = [(t, o) for t in far_first(nx) for o in (1, 0)] + [(0, 1)]

    loads = []
    for n, (source, target) in enumerate(
        (
            (rhs_hbm, rhs),
            (basis_hbm, basis),
            (dirichlet_hbm, dirichlet),
            (inverse_hbm, inverse),
            (schur_hbm, schur),
            (match_hbm, match),
            (cols_hbm, cols),
            (owner_hbm, owner),
        )
    ):
        copy = pltpu.make_async_copy(source, target, load_sem.at[n])
        copy.start()
        loads.append(copy)

    barrier = pltpu.get_barrier_semaphore()
    greeted = [line_x(t, o) for t, o in x_peers]
    greeted += [line_y(t) for t in far_first(ny)]
    greeted += [line_z(t) for t in far_first(nz)]
    greeted += [up, down]
    for peer in greeted:
        pl.semaphore_signal(barrier, inc=1, device_id=peer, device_id_type=MESH)

    for n in (5, 6, 7):
        loads[n].wait()
    at = [match[0, i] for i in range(HALF)]
    block_at = []
    for j in range(HALF):
        found = jnp.int32(0)
        for i in range(1, HALF):
            found = found + jnp.where(at[i] == j, jnp.int32(i), jnp.int32(0))
        block_at.append(found)
    block_at += [jnp.int32(b) for b in range(HALF, NB)]
    place_of = at + [jnp.int32(b) for b in range(HALF, NB)]

    for p in range(NB):
        b = block_at[p]
        table[p * KB] = b * KB
        for s in range(1, KB):
            c = cols[s, b]
            back = jnp.int32(0)
            for t in range(1, KB):
                back = back + jnp.where(cols[t, c] == b, jnp.int32(t), jnp.int32(0))
            table[p * KB + s] = c * KB + back

    loads[0].wait()
    for p in range(NB):
        faces[0, p] = rhs[block_at[p]]
    pl.semaphore_wait(barrier, len(greeted))

    def send_halo(stage):
        for side, peer in ((1, down), (0, up)):
            pltpu.make_async_remote_copy(
                src_ref=faces.at[stage, pl.ds(0 if side else HALF, HALF)],
                dst_ref=halo.at[stage, side],
                send_sem=halo_send_sem.at[stage],
                recv_sem=halo_sem.at[stage],
                device_id=peer,
                device_id_type=MESH,
            ).start()

    def whole(ref, send, recv):
        return pltpu.make_async_remote_copy(
            src_ref=ref, dst_ref=ref, send_sem=send, recv_sem=recv, device_id=up, device_id_type=MESH
        )

    def wait_halo(stage):
        whole(halo.at[stage], halo_send_sem.at[stage], halo_sem.at[stage]).wait_recv()

    def jump(stage):
        low = [faces[stage, p] - halo[stage, 0, p] for p in range(HALF)]
        high = [faces[stage, HALF + p] - halo[stage, 1, p] for p in range(HALF)]
        return low + high

    send_halo(0)

    lane = lax.broadcasted_iota(jnp.int32, (8, W), 1)
    lane_mode = lane // NJ
    lane_slot = lax.rem(lane, NJ)
    loads[1].wait()
    owners = [owner[0, block_at[p]].astype(F32) for p in range(NB)]
    for side in (0, 1):
        nb_send[side] = jnp.zeros((16, W), F32)
        for c in range(3):
            for j in range(HALF):
                p = j if side else HALF + j
                nb_send[side, c * HALF + j] = basis[c, block_at[p]]
        tag = jnp.zeros((8, W), F32)
        for j in range(HALF):
            p = j if side else HALF + j
            spot = NB + j + (HALF if side else 0)
            tag = jnp.where((lane_slot == spot) & (lane < LIVE), owners[p], tag)
        nb_send[side, 12] = tag[0]
    for side, peer in ((1, down), (0, up)):
        pltpu.make_async_remote_copy(
            src_ref=nb_send.at[side],
            dst_ref=nb_recv.at[side],
            send_sem=nb_send_sem,
            recv_sem=nb_sem,
            device_id=peer,
            device_id_type=MESH,
        ).start()

    def block_product(matrix, source):
        for b in range(NB):
            high, low = split(fields[source, place_of[b]])
            row = jnp.concatenate([high, low], axis=0)
            product = nn(row, jnp.concatenate([matrix[b, s] for s in range(KB)], axis=1))
            product = product[:LC] + product[LC:]
            for s in range(KB):
                parts[b * KB + s] = product[:, s * W : (s + 1) * W]
        result = []
        for p in range(NB):
            total = parts[table[p * KB]]
            for s in range(1, KB):
                total = total + parts[table[p * KB + s]]
            result.append(total)
        return result

    def inner(first, second):
        total = first[0] * second[0]
        for u, v in zip(first[1:], second[1:]):
            total = total + u * v
        return jnp.sum(total, axis=1, keepdims=True)

    wait_halo(0)
    residual = jump(0)
    for p in range(NB):
        fields[0, p] = residual[p] + residual[p]
    loads[2].wait()
    lifted = block_product(dirichlet, 0)
    for p in range(NB):
        faces[1, p] = lifted[p]
    send_halo(1)
    rz0 = inner([fields[0, p] for p in range(NB)], lifted)

    whole(nb_recv, nb_send_sem, nb_sem).wait_recv()
    own_lanes = nb_recv[0, pl.ds(12, 1)] + nb_recv[1, pl.ds(12, 1)]
    own_lanes = jnp.broadcast_to(own_lanes, (8, W))
    for p in range(NB):
        own_lanes = jnp.where((lane_slot == p) & (lane < LIVE), owners[p], own_lanes)
    own_lanes = jnp.where(lane < LIVE, own_lanes, -1.0)
    own_send[0] = own_lanes[:4]
    own_send[1] = pltpu.roll(own_lanes, 64, 1)[:4]
    own_recv[0] = own_lanes[:4]
    for t, o in x_peers:
        pltpu.make_async_remote_copy(
            src_ref=own_send.at[o],
            dst_ref=own_recv.at[2 * t + o],
            send_sem=own_send_sem,
            recv_sem=own_sem,
            device_id=line_x(t, o),
            device_id_type=MESH,
        ).start()

    rows = []
    for c in range(3):
        rows += [basis[c, pl.ds(block_at[p], 1)] for p in range(HALF)]
        rows.append(basis[c, HALF:NB])
        rows.append(-nb_recv[0, c * HALF : (c + 1) * HALF])
        rows.append(-nb_recv[1, c * HALF : (c + 1) * HALF])
    rows = jnp.concatenate(rows + [jnp.zeros((W - LIVE, W), F32)], axis=0)
    row_place = lax.rem(lax.broadcasted_iota(jnp.int32, (W, W), 0), NB)
    for p in range(NB):
        high, low = split(jnp.where(row_place == p, rows, 0.0))
        spread[0, :, p * W : (p + 1) * W] = high
        spread[1, :, p * W : (p + 1) * W] = low

    def send_corner_sums(turn, lifted):
        doubled = jnp.concatenate([u + u for u in lifted], axis=1)
        high, low = split(doubled)
        first = nt(jnp.concatenate([high, low], axis=0), spread[0])
        sums = first[:LC] + first[LC:] + nt(high, spread[1])
        rolled = pltpu.roll(sums, 64, 1)
        mine = jnp.where(core == 0, sums[:4], sums[4:])
        a_send[turn, 0] = mine
        a_send[turn, 1] = jnp.where(core == 0, rolled[4:], rolled[:4])
        a_recv[turn, 0] = mine
        for t, o in x_peers:
            pltpu.make_async_remote_copy(
                src_ref=a_send.at[turn, o],
                dst_ref=a_recv.at[turn, 2 * t + o],
                send_sem=a_send_sem.at[turn],
                recv_sem=a_sem.at[turn],
                device_id=line_x(t, o),
                device_id_type=MESH,
            ).start()

    def pair(ref):
        high = ref.astype(BF16).astype(F32)
        return jnp.concatenate([high, ref - high], axis=0).astype(BF16)

    def assemble(turn, scalars):
        whole(a_recv.at[turn, pl.ds(1, 2 * nx - 1)], a_send_sem.at[turn], a_sem.at[turn]).wait_recv()
        came = jnp.concatenate([a_recv[turn, 2 * t] + a_recv[turn, 2 * t + 1] for t in range(nx)], axis=1)
        dense = nt(pair(came), onehot[...])
        dense = dense[:4] + dense[4:]
        b_recv[turn, 0, 0] = jnp.concatenate([dense[:, :W], dense[:, W : 2 * W]], axis=0)
        b_recv[turn, 0, 1] = jnp.concatenate([dense[:, 2 * W :], scalars], axis=0)
        for t in far_first(ny):
            pltpu.make_async_remote_copy(
                src_ref=b_recv.at[turn, 0],
                dst_ref=b_recv.at[turn, t],
                send_sem=b_send_sem.at[turn],
                recv_sem=b_sem.at[turn],
                device_id=line_y(t),
                device_id_type=MESH,
            ).start()

    def total_of(ref, turn, count):
        sums = []
        for h in range(2):
            total = ref[turn, 0, h]
            for t in range(1, count):
                total = total + ref[turn, t, h]
            sums.append(total)
        return sums

    def across_z(turn):
        whole(b_recv.at[turn, pl.ds(1, ny - 1)], b_send_sem.at[turn], b_sem.at[turn]).wait_recv()
        for h, total in enumerate(total_of(b_recv, turn, ny)):
            c_recv[turn, 0, h] = total
        for t in far_first(nz):
            pltpu.make_async_remote_copy(
                src_ref=c_recv.at[turn, 0],
                dst_ref=c_recv.at[turn, t],
                send_sem=c_send_sem.at[turn],
                recv_sem=c_sem.at[turn],
                device_id=line_z(t),
                device_id_type=MESH,
            ).start()

    def solve(turn):
        whole(c_recv.at[turn, pl.ds(1, nz - 1)], c_send_sem.at[turn], c_sem.at[turn]).wait_recv()
        first, second = total_of(c_recv, turn, nz)
        summed = jnp.concatenate([first[:4], first[4:], second[:4]], axis=1)
        lhs = pair(summed)
        solved = nn(lhs, inv_split[0])
        solved = solved[:4] + solved[4:] + nn(lhs, inv_split[1])[:4]
        energy = jnp.sum(summed * solved, axis=1, keepdims=True)
        chosen = nn(pair(solved), onehot[...])
        chosen = chosen[:4] + chosen[4:]
        lane4 = lane[:4]
        extra = jnp.where(lane4 == LANE_ENERGY, energy, second[4:])
        aside = (lane4 >= LANE_ENERGY) & (lane4 < 64)
        for t in range(nx):
            d_send[turn, t] = jnp.where(aside, extra, chosen[:, t * W : (t + 1) * W])
        d_recv[turn, 0] = d_send[turn, 0]
        for t, o in x_peers:
            pltpu.make_async_remote_copy(
                src_ref=d_send.at[turn, t],
                dst_ref=d_recv.at[turn, 2 * t + o],
                send_sem=d_send_sem.at[turn],
                recv_sem=d_sem.at[turn],
                device_id=line_x(nx - t, o),
                device_id_type=MESH,
            ).start()

    def gathered(turn):
        whole(d_recv.at[turn, pl.ds(1, 2 * nx - 1)], d_send_sem.at[turn], d_sem.at[turn]).wait_recv()
        same, other = d_recv[turn, 0], d_recv[turn, 1]
        for t in range(1, nx):
            same = same + d_recv[turn, 2 * t]
            other = other + d_recv[turn, 2 * t + 1]
        both = jnp.where(
            core == 0, jnp.concatenate([same, other], axis=0), jnp.concatenate([other, same], axis=0)
        )
        turned = pltpu.roll(both, 64, 1)
        row_core = lax.broadcasted_iota(jnp.int32, (8, W), 0) // 4
        values = jnp.where(lane < LIVE, jnp.where(row_core == core, both, turned), 0.0)
        high, low = split(values)
        mixed = nn(jnp.concatenate([high, low], axis=0), spread[0])
        mixed = mixed[:LC] + mixed[LC:] + nn(high, spread[1])
        return [mixed[:, p * W : (p + 1) * W] for p in range(NB)], both, same + other

    send_corner_sums(0, lifted)

    whole(own_recv.at[pl.ds(1, 2 * nx - 1)], own_send_sem, own_sem).wait_recv()
    corner = lax.broadcasted_iota(jnp.int32, (W, W), 0).astype(F32)
    base = (g * W).astype(F32)
    lane1 = lane[:1]
    for t in range(nx):
        ids = jnp.where(lane1 < 64, own_recv[2 * t, pl.ds(0, 1)], own_recv[2 * t + 1, pl.ds(0, 1)]) - base
        for c in range(3):
            masked = jnp.where(lax.rem(lane1, 64) // NJ == c, ids, -1.0)
            onehot[c * W : (c + 1) * W, t * W : (t + 1) * W] = jnp.where(corner == masked, 1.0, 0.0).astype(BF16)

    assemble(0, jnp.zeros((4, W), F32))

    def apply_schur(stage, source):
        wait_halo(stage - 1)
        for p, value in enumerate(jump(stage - 1)):
            fields[source, p] = value + value
        product = block_product(schur, source)
        for p in range(NB):
            faces[stage, p] = product[p]
        send_halo(stage)
        return product

    loads[4].wait()
    apply_schur(2, 1)
    across_z(0)
    loads[3].wait()
    high, low = split(inverse[...])
    inv_split[0] = high
    inv_split[1] = low
    solve(0)
    mixed, _, _ = gathered(0)
    wait_halo(2)
    image = [u + v for u, v in zip(jump(2), mixed)]
    for p in range(NB):
        fields[2, p] = image[p] + image[p]

    lifted = block_product(dirichlet, 2)
    for p in range(NB):
        faces[3, p] = lifted[p]
    send_halo(3)
    send_corner_sums(1, lifted)
    doubled = [fields[2, p] for p in range(NB)]
    g1 = inner([fields[1, p] for p in range(NB)], doubled) * 0.25
    m1 = inner(doubled, lifted)
    product = apply_schur(4, 3)
    h1 = inner([fields[3, p] for p in range(NB)], product)
    lane_of = LANE_SCAL
    scalars = jnp.zeros((8, W), F32)
    row_half = lax.broadcasted_iota(jnp.int32, (8, W), 0) // 4
    for n, value in enumerate((rz0, g1, m1, h1)):
        scalars = jnp.where(lane == lane_of + n + 4 * row_half, value, scalars)
    assemble(1, scalars[:4] + scalars[4:])
    across_z(1)
    solve(1)
    mixed, both, sums = gathered(1)

    def pick(n):
        low = jnp.sum(jnp.where(lane[:4] == LANE_SCAL + n, sums, 0.0), axis=1, keepdims=True)
        high = jnp.sum(jnp.where(lane[:4] == LANE_SCAL + 4 + n, sums, 0.0), axis=1, keepdims=True)
        return jnp.concatenate([low, high], axis=0)

    rz0, g1, m1, h1 = (pick(n) for n in range(4))
    h1 = h1 + jnp.sum(jnp.where(lane == LANE_ENERGY, both, 0.0), axis=1, keepdims=True)
    alpha0 = rz0 / g1
    rz1 = alpha0 * alpha0 * m1 - rz0
    grow = 1.0 + rz1 / rz0
    energy = grow * grow * g1 - 2.0 * grow * alpha0 * m1 + alpha0 * alpha0 * h1
    alpha1 = rz1 / energy
    first = alpha0 + alpha1 * grow
    second = -alpha1 * alpha0
    wait_halo(4)
    last = [u + v for u, v in zip(jump(4), mixed)]
    for p in range(NB):
        parts[p] = 0.5 * (first * fields[1, p] + second * fields[3, p])
        parts[NB + p] = 0.5 * (fields[0, p] - first * fields[2, p]) - second * last[p]
    for b in range(NB):
        dual_out[b] = parts[place_of[b]]
        residual_out[b] = parts[place_of[b] + NB]

    for stage in range(5):
        whole(halo.at[stage], halo_send_sem.at[stage], halo_sem.at[stage]).wait_send()
    whole(nb_send, nb_send_sem, nb_sem).wait_send()
    whole(own_recv.at[pl.ds(1, 2 * nx - 1)], own_send_sem, own_sem).wait_send()
    for turn in (0, 1):
        whole(a_recv.at[turn, pl.ds(1, 2 * nx - 1)], a_send_sem.at[turn], a_sem.at[turn]).wait_send()
        whole(b_recv.at[turn, pl.ds(1, ny - 1)], b_send_sem.at[turn], b_sem.at[turn]).wait_send()
        whole(c_recv.at[turn, pl.ds(1, nz - 1)], c_send_sem.at[turn], c_sem.at[turn]).wait_send()
        whole(d_recv.at[turn, pl.ds(1, 2 * nx - 1)], d_send_sem.at[turn], d_sem.at[turn]).wait_send()


def shards(
    sizes,
    jump_rhs,
    schur_blocks,
    dirichlet_blocks,
    block_columns,
    face_partner_slots,
    corner_basis,
    corner_owner,
    coarse_inverse,
):
    ny, nz, nx = sizes
    field = pltpu.VMEM((NB, LC, W), F32)
    far = pl.BlockSpec(memory_space=pl.ANY)
    near = pl.BlockSpec(memory_space=pltpu.VMEM)
    dma = pltpu.SemaphoreType.DMA
    dual, residual = pl.pallas_call(
        functools.partial(kernel, sizes),
        out_shape=(field, field),
        in_specs=[far] * 8,
        out_specs=(near, near),
        scratch_shapes=[
            pltpu.SMEM((KB, NB), jnp.int32),
            pltpu.SMEM((1, HALF), jnp.int32),
            pltpu.SMEM((1, NB), jnp.int32),
            pltpu.VMEM((NB, LC, W), F32),
            pltpu.VMEM((NB, KB, W, W), BF16),
            pltpu.VMEM((NB, KB, W, W), BF16),
            pltpu.VMEM((3, NB, W), F32),
            pltpu.VMEM((3 * W, 3 * W), F32),
            pltpu.SMEM((NB * KB,), jnp.int32),
            pltpu.VMEM((NB * KB, LC, W), F32),
            pltpu.VMEM((5, NB, LC, W), F32),
            pltpu.VMEM((5, 2, HALF, LC, W), F32),
            pltpu.VMEM((2, 16, W), F32),
            pltpu.VMEM((2, 16, W), F32),
            pltpu.VMEM((2, W, NB * W), BF16),
            pltpu.VMEM((2, 4, W), F32),
            pltpu.VMEM((2 * nx, 4, W), F32),
            pltpu.VMEM((3 * W, nx * W), BF16),
            pltpu.VMEM((2, 3 * W, 3 * W), BF16),
            pltpu.VMEM((2, 2, 4, W), F32),
            pltpu.VMEM((2, 2 * nx, 4, W), F32),
            pltpu.VMEM((2, ny, 2, 8, W), F32),
            pltpu.VMEM((2, nz, 2, 8, W), F32),
            pltpu.VMEM((2, nx, 4, W), F32),
            pltpu.VMEM((2, 2 * nx, 4, W), F32),
            pltpu.VMEM((4, NB, LC, W), F32),
            dma((8,)),
            dma((5,)),
            dma((5,)),
            dma(()),
            dma(()),
            dma(()),
            dma(()),
            dma((2,)),
            dma((2,)),
            dma((2,)),
            dma((2,)),
            dma((2,)),
            dma((2,)),
            dma((2,)),
            dma((2,)),
        ],
        compiler_params=pltpu.CompilerParams(
            collective_id=0, has_side_effects=True, vmem_limit_bytes=60 * 1024 * 1024
        ),
    )(
        block_columns[0, 0].T,
        face_partner_slots[0],
        corner_owner[0],
        jump_rhs[0, 0],
        schur_blocks[0, 0],
        dirichlet_blocks[0, 0],
        corner_basis[:, 0, 0],
        coarse_inverse[0],
    )
    return dual[None, None], residual[None, None]


def solution(mesh):
    sizes = plan(mesh.shape["sub"], mesh.shape["grp"])
    placed = (
        P("grp", "sub", None, None, None),
        P("grp", "sub", None, None, None, None),
        P("grp", "sub", None, None, None, None),
        P("grp", "sub", None, None),
        P("grp", "sub", None),
        P(None, "grp", "sub", None, None),
        P("grp", "sub", None),
        P("grp", None, None),
    )
    return jax.shard_map(
        functools.partial(shards, sizes),
        mesh=mesh,
        in_specs=placed,
        out_specs=(P("grp", "sub", None, None, None), P("grp", "sub", None, None, None)),
        check_vma=False,
    )
```

```python
import functools

import jax
import jax.numpy as jnp
from jax import lax
from jax.experimental import pallas as pl
from jax.experimental.pallas import tpu as pltpu
from jax.sharding import PartitionSpec as P

MESH = pl.DeviceIdType.MESH
F32 = jnp.float32
BF16 = jnp.bfloat16
W = 128
LC = 8
NB = 8
HALF = 4
KB = 4
NJ = 16
LIVE = 3 * NJ
LANE_ENERGY = 48


def plan(sub_count, grp_count):
    chips = sub_count // 2
    along_z = 1
    while along_z * along_z < chips:
        along_z *= 2
    return chips // along_z, along_z, grp_count


def far_first(count):
    return sorted(range(1, count), key=lambda t: -min(t, count - t))


def split(x):
    high = x.astype(BF16)
    low = (x - high.astype(F32)).astype(BF16)
    return high, low


def nn(a, b):
    return lax.dot_general(a, b, (((1,), (0,)), ((), ())), preferred_element_type=F32)


def nt(a, b):
    return lax.dot_general(a, b, (((1,), (1,)), ((), ())), preferred_element_type=F32)


def kernel(
    sizes,
    cols_hbm,
    match_hbm,
    owner_hbm,
    rhs_hbm,
    schur_hbm,
    dirichlet_hbm,
    basis_hbm,
    inverse_hbm,
    dual_out,
    residual_out,
    cols,
    match,
    owner,
    rhs,
    schur,
    dirichlet,
    basis,
    inverse,
    table,
    parts,
    faces,
    halo,
    nb_send,
    nb_recv,
    spread,
    own_send,
    own_recv,
    onehot,
    inv_split,
    a_send,
    a_recv,
    b_recv,
    c_recv,
    d_send,
    d_recv,
    fields,
    kparts,
    moved,
    k_send,
    k_recv,
    k_pair,
    x_send,
    x_recv,
    s_y,
    s_z,
    s_x,
    load_sem,
    halo_send_sem,
    halo_sem,
    nb_send_sem,
    nb_sem,
    own_send_sem,
    own_sem,
    a_send_sem,
    a_sem,
    b_send_sem,
    b_sem,
    c_send_sem,
    c_sem,
    d_send_sem,
    d_sem,
    k_send_sem,
    k_sem,
    x_send_sem,
    x_sem,
    s_send_sem,
    s_sem,
):
    ny, nz, nx = sizes
    strips = ny * nz * 2
    k = lax.axis_index("sub")
    g = lax.axis_index("grp")
    core = lax.rem(k, 2)
    zi = lax.rem(k // 2, nz)
    yi = k // (2 * nz)

    def dev(sub, grp):
        return {"sub": sub, "grp": grp}

    up = dev(lax.rem(k + 1, strips), g)
    down = dev(lax.rem(k + strips - 1, strips), g)

    def line_x(step, other):
        sub = (k + 1 - 2 * core) if other else k
        return dev(sub, lax.rem(g + step, nx))

    def line_y(step):
        return dev((lax.rem(yi + step, ny) * nz + zi) * 2 + core, g)

    def line_yc(step, other):
        c = 1 - core if other else core
        return dev((lax.rem(yi + step, ny) * nz + zi) * 2 + c, g)

    def line_z(step):
        return dev((yi * nz + lax.rem(zi + step, nz)) * 2 + core, g)

    x_peers = [(t, o) for t in far_first(nx) for o in (1, 0)] + [(0, 1)]
    yc_peers = [(t, o) for t in far_first(ny) for o in (1, 0)] + [(0, 1)]

    loads = []
    for n, (source, target) in enumerate(
        (
            (rhs_hbm, rhs),
            (basis_hbm, basis),
            (dirichlet_hbm, dirichlet),
            (inverse_hbm, inverse),
            (schur_hbm, schur),
            (match_hbm, match),
            (cols_hbm, cols),
            (owner_hbm, owner),
        )
    ):
        copy = pltpu.make_async_copy(source, target, load_sem.at[n])
        copy.start()
        loads.append(copy)

    barrier = pltpu.get_barrier_semaphore()
    greeted = [line_x(t, o) for t, o in x_peers]
    greeted += [line_yc(t, o) for t, o in yc_peers[:-1]]
    greeted += [line_z(t) for t in far_first(nz)]
    greeted += [up, down]
    for peer in greeted:
        pl.semaphore_signal(barrier, inc=1, device_id=peer, device_id_type=MESH)

    for n in (5, 6, 7):
        loads[n].wait()
    at = [match[0, i] for i in range(HALF)]
    block_at = []
    for j in range(HALF):
        found = jnp.int32(0)
        for i in range(1, HALF):
            found = found + jnp.where(at[i] == j, jnp.int32(i), jnp.int32(0))
        block_at.append(found)
    block_at += [jnp.int32(b) for b in range(HALF, NB)]
    place_of = at + [jnp.int32(b) for b in range(HALF, NB)]

    for p in range(NB):
        b = block_at[p]
        table[p * KB] = b * KB
        for s in range(1, KB):
            c = cols[s, b]
            back = jnp.int32(0)
            for t in range(1, KB):
                back = back + jnp.where(cols[t, c] == b, jnp.int32(t), jnp.int32(0))
            table[p * KB + s] = c * KB + back

    loads[0].wait()
    for p in range(NB):
        faces[0, p] = rhs[block_at[p]]
    pl.semaphore_wait(barrier, len(greeted))

    def send_halo(stage):
        for side, peer in ((1, down), (0, up)):
            pltpu.make_async_remote_copy(
                src_ref=faces.at[stage, pl.ds(0 if side else HALF, HALF)],
                dst_ref=halo.at[stage, side],
                send_sem=halo_send_sem.at[stage],
                recv_sem=halo_sem.at[stage],
                device_id=peer,
                device_id_type=MESH,
            ).start()

    def whole(ref, send, recv):
        return pltpu.make_async_remote_copy(
            src_ref=ref, dst_ref=ref, send_sem=send, recv_sem=recv, device_id=up, device_id_type=MESH
        )

    def wait_halo(stage):
        whole(halo.at[stage], halo_send_sem.at[stage], halo_sem.at[stage]).wait_recv()

    def jump(stage):
        low = [faces[stage, p] - halo[stage, 0, p] for p in range(HALF)]
        high = [faces[stage, HALF + p] - halo[stage, 1, p] for p in range(HALF)]
        return low + high

    send_halo(0)

    lane = lax.broadcasted_iota(jnp.int32, (8, W), 1)
    lane_mode = lane // NJ
    lane_slot = lax.rem(lane, NJ)
    loads[1].wait()
    owners = [owner[0, block_at[p]].astype(F32) for p in range(NB)]
    for side in (0, 1):
        nb_send[side] = jnp.zeros((16, W), F32)
        for c in range(3):
            for j in range(HALF):
                p = j if side else HALF + j
                nb_send[side, c * HALF + j] = basis[c, block_at[p]]
        tag = jnp.zeros((8, W), F32)
        for j in range(HALF):
            p = j if side else HALF + j
            spot = NB + j + (HALF if side else 0)
            tag = jnp.where((lane_slot == spot) & (lane < LIVE), owners[p], tag)
        nb_send[side, 12] = tag[0]
    for side, peer in ((1, down), (0, up)):
        pltpu.make_async_remote_copy(
            src_ref=nb_send.at[side],
            dst_ref=nb_recv.at[side],
            send_sem=nb_send_sem,
            recv_sem=nb_sem,
            device_id=peer,
            device_id_type=MESH,
        ).start()

    def block_product(matrix, source):
        for b in range(NB):
            high, low = split(fields[source, place_of[b]])
            row = jnp.concatenate([high, low], axis=0)
            product = nn(row, jnp.concatenate([matrix[b, s] for s in range(KB)], axis=1))
            product = product[:LC] + product[LC:]
            for s in range(KB):
                parts[b * KB + s] = product[:, s * W : (s + 1) * W]
        result = []
        for p in range(NB):
            total = parts[table[p * KB]]
            for s in range(1, KB):
                total = total + parts[table[p * KB + s]]
            result.append(total)
        return result

    def inner(first, second):
        total = first[0] * second[0]
        for u, v in zip(first[1:], second[1:]):
            total = total + u * v
        return jnp.sum(total, axis=1, keepdims=True)

    wait_halo(0)
    residual = jump(0)
    for p in range(NB):
        fields[0, p] = residual[p] + residual[p]
    loads[2].wait()
    lifted = block_product(dirichlet, 0)
    for p in range(NB):
        faces[1, p] = lifted[p]
    send_halo(1)
    rz0 = inner([fields[0, p] for p in range(NB)], lifted)

    whole(nb_recv, nb_send_sem, nb_sem).wait_recv()
    own_lanes = nb_recv[0, pl.ds(12, 1)] + nb_recv[1, pl.ds(12, 1)]
    own_lanes = jnp.broadcast_to(own_lanes, (8, W))
    for p in range(NB):
        own_lanes = jnp.where((lane_slot == p) & (lane < LIVE), owners[p], own_lanes)
    own_lanes = jnp.where(lane < LIVE, own_lanes, -1.0)
    own_send[0] = own_lanes[:4]
    own_send[1] = pltpu.roll(own_lanes, 64, 1)[:4]
    own_recv[0] = own_lanes[:4]
    for t, o in x_peers:
        pltpu.make_async_remote_copy(
            src_ref=own_send.at[o],
            dst_ref=own_recv.at[2 * t + o],
            send_sem=own_send_sem,
            recv_sem=own_sem,
            device_id=line_x(t, o),
            device_id_type=MESH,
        ).start()

    rows = []
    for c in range(3):
        rows += [basis[c, pl.ds(block_at[p], 1)] for p in range(HALF)]
        rows.append(basis[c, HALF:NB])
        rows.append(-nb_recv[0, c * HALF : (c + 1) * HALF])
        rows.append(-nb_recv[1, c * HALF : (c + 1) * HALF])
    rows = jnp.concatenate(rows + [jnp.zeros((W - LIVE, W), F32)], axis=0)
    row_place = lax.rem(lax.broadcasted_iota(jnp.int32, (W, W), 0), NB)
    for p in range(NB):
        high, low = split(jnp.where(row_place == p, rows, 0.0))
        spread[0, p] = high
        spread[1, p] = low

    def wide(ref, n):
        return jnp.concatenate([ref[n, p] for p in range(NB)], axis=1)

    def send_corner_sums(turn, lifted):
        doubled = jnp.concatenate([u + u for u in lifted], axis=1)
        high, low = split(doubled)
        first = nt(jnp.concatenate([high, low], axis=0), wide(spread, 0))
        sums = first[:LC] + first[LC:] + nt(high, wide(spread, 1))
        rolled = pltpu.roll(sums, 64, 1)
        mine = jnp.where(core == 0, sums[:4], sums[4:])
        a_send[turn, 0] = mine
        a_send[turn, 1] = jnp.where(core == 0, rolled[4:], rolled[:4])
        a_recv[turn, 0] = mine
        for t, o in x_peers:
            pltpu.make_async_remote_copy(
                src_ref=a_send.at[turn, o],
                dst_ref=a_recv.at[turn, 2 * t + o],
                send_sem=a_send_sem.at[turn],
                recv_sem=a_sem.at[turn],
                device_id=line_x(t, o),
                device_id_type=MESH,
            ).start()

    def pair(ref):
        high = ref.astype(BF16).astype(F32)
        return jnp.concatenate([high, ref - high], axis=0).astype(BF16)

    def assemble(turn):
        whole(a_recv.at[turn, pl.ds(1, 2 * nx - 1)], a_send_sem.at[turn], a_sem.at[turn]).wait_recv()
        tiles = [a_recv[turn, 2 * t] + a_recv[turn, 2 * t + 1] for t in range(nx)]
        if turn:
            whole(x_recv.at[pl.ds(1, nx - 1)], x_send_sem, x_sem).wait_recv()
            tiles = [u + x_send[t] for t, u in enumerate(tiles)]
            for d in range(1, nx):
                tiles = [u + x_recv[d, t] for t, u in enumerate(tiles)]
        came = jnp.concatenate(tiles, axis=1)
        dense = nt(pair(came), onehot[...])
        dense = dense[:4] + dense[4:]
        b_recv[turn, 0, 0] = jnp.concatenate([dense[:, :W], dense[:, W : 2 * W]], axis=0)
        b_recv[turn, 0, 1] = jnp.concatenate([dense[:, 2 * W :], jnp.zeros((4, W), F32)], axis=0)
        for t in far_first(ny):
            pltpu.make_async_remote_copy(
                src_ref=b_recv.at[turn, 0],
                dst_ref=b_recv.at[turn, t],
                send_sem=b_send_sem.at[turn],
                recv_sem=b_sem.at[turn],
                device_id=line_y(t),
                device_id_type=MESH,
            ).start()

    def total_of(ref, turn, count):
        sums = []
        for h in range(2):
            total = ref[turn, 0, h]
            for t in range(1, count):
                total = total + ref[turn, t, h]
            sums.append(total)
        return sums

    def across_z(turn):
        whole(b_recv.at[turn, pl.ds(1, ny - 1)], b_send_sem.at[turn], b_sem.at[turn]).wait_recv()
        for h, total in enumerate(total_of(b_recv, turn, ny)):
            c_recv[turn, 0, h] = total
        for t in far_first(nz):
            pltpu.make_async_remote_copy(
                src_ref=c_recv.at[turn, 0],
                dst_ref=c_recv.at[turn, t],
                send_sem=c_send_sem.at[turn],
                recv_sem=c_sem.at[turn],
                device_id=line_z(t),
                device_id_type=MESH,
            ).start()

    def solve(turn):
        whole(c_recv.at[turn, pl.ds(1, nz - 1)], c_send_sem.at[turn], c_sem.at[turn]).wait_recv()
        first, second = total_of(c_recv, turn, nz)
        summed = jnp.concatenate([first[:4], first[4:], second[:4]], axis=1)
        lhs = pair(summed)
        solved = nn(lhs, inv_split[0])
        solved = solved[:4] + solved[4:] + nn(lhs, inv_split[1])[:4]
        energy = jnp.sum(summed * solved, axis=1, keepdims=True)
        chosen = nn(pair(solved), onehot[...])
        chosen = chosen[:4] + chosen[4:]
        lane4 = lane[:4]
        for t in range(nx):
            d_send[turn, t] = jnp.where(lane4 == LANE_ENERGY, energy, chosen[:, t * W : (t + 1) * W])
        d_recv[turn, 0] = d_send[turn, 0]
        for t, o in x_peers:
            pltpu.make_async_remote_copy(
                src_ref=d_send.at[turn, t],
                dst_ref=d_recv.at[turn, 2 * t + o],
                send_sem=d_send_sem.at[turn],
                recv_sem=d_sem.at[turn],
                device_id=line_x(nx - t, o),
                device_id_type=MESH,
            ).start()
        return chosen

    def gathered(turn):
        whole(d_recv.at[turn, pl.ds(1, 2 * nx - 1)], d_send_sem.at[turn], d_sem.at[turn]).wait_recv()
        same, other = d_recv[turn, 0], d_recv[turn, 1]
        for t in range(1, nx):
            same = same + d_recv[turn, 2 * t]
            other = other + d_recv[turn, 2 * t + 1]
        both = jnp.where(
            core == 0, jnp.concatenate([same, other], axis=0), jnp.concatenate([other, same], axis=0)
        )
        turned = pltpu.roll(both, 64, 1)
        row_core = lax.broadcasted_iota(jnp.int32, (8, W), 0) // 4
        values = jnp.where(lane < LIVE, jnp.where(row_core == core, both, turned), 0.0)
        high, low = split(values)
        return high, low, both

    def expand(high, low, ref):
        mixed = nn(jnp.concatenate([high, low], axis=0), wide(ref, 0))
        mixed = mixed[:LC] + mixed[LC:] + nn(high, wide(ref, 1))
        return [mixed[:, p * W : (p + 1) * W] for p in range(NB)]

    send_corner_sums(0, lifted)

    whole(own_recv.at[pl.ds(1, 2 * nx - 1)], own_send_sem, own_sem).wait_recv()
    corner = lax.broadcasted_iota(jnp.int32, (W, W), 0).astype(F32)
    base = (g * W).astype(F32)
    lane1 = lane[:1]
    for t in range(nx):
        ids = jnp.where(lane1 < 64, own_recv[2 * t, pl.ds(0, 1)], own_recv[2 * t + 1, pl.ds(0, 1)]) - base
        for c in range(3):
            masked = jnp.where(lax.rem(lane1, 64) // NJ == c, ids, -1.0)
            onehot[c * W : (c + 1) * W, t * W : (t + 1) * W] = jnp.where(corner == masked, 1.0, 0.0).astype(BF16)

    for b in range(NB):
        p = place_of[b]
        row = jnp.concatenate([spread[0, p][:LIVE], spread[1, p][:LIVE]], axis=0)
        product = nn(row, jnp.concatenate([dirichlet[b, n] for n in range(KB)], axis=1))
        product = product[:LIVE] + product[LIVE:]
        for n in range(KB):
            kparts[b * KB + n] = product[:, n * W : (n + 1) * W]
    blank = jnp.zeros((W - LIVE, W), F32)
    for p in range(NB):
        total = kparts[table[p * KB]]
        for n in range(1, KB):
            total = total + kparts[table[p * KB + n]]
        high, low = split(jnp.concatenate([total, blank], axis=0))
        moved[0, p] = high
        moved[1, p] = low
    high, low = wide(moved, 0)[:LIVE], wide(moved, 1)[:LIVE]
    first = nt(jnp.concatenate([high, low], axis=0), wide(spread, 0))
    coupling = 4.0 * (first[:LIVE] + first[LIVE:] + nt(high, wide(spread, 1)))
    k_send[0] = coupling
    k_send[1] = pltpu.roll(coupling, 64, 1)
    k_recv[0] = coupling
    for t, o in x_peers:
        pltpu.make_async_remote_copy(
            src_ref=k_send.at[o],
            dst_ref=k_recv.at[2 * t + o],
            send_sem=k_send_sem,
            recv_sem=k_sem,
            device_id=line_x(t, o),
            device_id_type=MESH,
        ).start()

    def apply_schur(stage, source):
        wait_halo(stage - 1)
        for p, value in enumerate(jump(stage - 1)):
            fields[source, p] = value + value
        product = block_product(schur, source)
        for p in range(NB):
            faces[stage, p] = product[p]
        send_halo(stage)
        return product

    loads[4].wait()
    apply_schur(2, 1)
    assemble(0)

    wait_halo(2)
    for p, value in enumerate(jump(2)):
        fields[2, p] = value + value
    lifted = block_product(dirichlet, 2)
    for p in range(NB):
        faces[3, p] = lifted[p]
    send_corner_sums(1, lifted)
    loads[3].wait()
    high, low = split(inverse[...])
    inv_split[0] = high
    inv_split[1] = low
    across_z(0)
    whole(k_recv.at[pl.ds(1, 2 * nx - 1)], k_send_sem, k_sem).wait_recv()
    gap = jnp.zeros((64 - LIVE, W), F32)
    for t in range(nx):
        high, low = split(jnp.concatenate([k_recv[2 * t], gap, k_recv[2 * t + 1], gap], axis=0))
        k_pair[0, t] = high
        k_pair[1, t] = low

    chosen = pair(solve(0))
    for t in range(nx):
        tile = chosen[:, t * W : (t + 1) * W]
        both = nn(tile, k_pair[0, t])
        both = both[:4] + both[4:] + nn(tile, k_pair[1, t])[:4]
        x_send[t] = both
        x_send[nx + t] = both
    for d in far_first(nx):
        pltpu.make_async_remote_copy(
            src_ref=x_send.at[pl.ds(nx - d, nx)],
            dst_ref=x_recv.at[d],
            send_sem=x_send_sem,
            recv_sem=x_sem,
            device_id=line_x(d, 0),
            device_id_type=MESH,
        ).start()

    high, low, _ = gathered(0)
    for p, value in enumerate(expand(high, low, moved)):
        faces[3, p] = faces[3, p] + (value + value)
    send_halo(3)
    for p, value in enumerate(expand(high, low, spread)):
        fields[2, p] = fields[2, p] + (value + value)
    doubled = [fields[2, p] for p in range(NB)]
    g1 = inner([fields[1, p] for p in range(NB)], doubled) * 0.25
    m1 = inner(doubled, [faces[3, p] for p in range(NB)])
    assemble(1)

    product = apply_schur(4, 3)
    h1 = inner([fields[3, p] for p in range(NB)], product)
    scalars = jnp.zeros((8, W), F32)
    for n, value in enumerate((rz0, g1, m1, h1)):
        scalars = jnp.where(lane == n, value, scalars)

    def share(ref, step, peers, value):
        ref[0] = value
        for slot, peer in peers:
            pltpu.make_async_remote_copy(
                src_ref=ref.at[0],
                dst_ref=ref.at[slot],
                send_sem=s_send_sem.at[step],
                recv_sem=s_sem.at[step],
                device_id=peer,
                device_id_type=MESH,
            ).start()

    def shared(ref, step, count):
        whole(ref.at[pl.ds(1, count - 1)], s_send_sem.at[step], s_sem.at[step]).wait_recv()
        total = ref[0]
        for n in range(1, count):
            total = total + ref[n]
        return total

    share(s_y, 0, [(2 * t + o, line_yc(t, o)) for t, o in yc_peers], scalars)
    across_z(1)
    share(s_z, 1, [(t, line_z(t)) for t in far_first(nz)], shared(s_y, 0, 2 * ny))
    solve(1)
    share(s_x, 2, [(t, line_x(t, 0)) for t in far_first(nx)], shared(s_z, 1, nz))
    high, low, both = gathered(1)
    mixed = expand(high, low, spread)
    sums = shared(s_x, 2, nx)

    def pick(n):
        return jnp.sum(jnp.where(lane == n, sums, 0.0), axis=1, keepdims=True)

    rz0, g1, m1, h1 = (pick(n) for n in range(4))
    h1 = h1 + jnp.sum(jnp.where(lane == LANE_ENERGY, both, 0.0), axis=1, keepdims=True)
    alpha0 = rz0 / g1
    rz1 = alpha0 * alpha0 * m1 - rz0
    grow = 1.0 + rz1 / rz0
    energy = grow * grow * g1 - 2.0 * grow * alpha0 * m1 + alpha0 * alpha0 * h1
    alpha1 = rz1 / energy
    first = alpha0 + alpha1 * grow
    second = -alpha1 * alpha0
    wait_halo(4)
    last = [u + v for u, v in zip(jump(4), mixed)]
    for p in range(NB):
        parts[p] = 0.5 * (first * fields[1, p] + second * fields[3, p])
        parts[NB + p] = 0.5 * (fields[0, p] - first * fields[2, p]) - second * last[p]
    for b in range(NB):
        dual_out[b] = parts[place_of[b]]
        residual_out[b] = parts[place_of[b] + NB]

    for stage in range(5):
        whole(halo.at[stage], halo_send_sem.at[stage], halo_sem.at[stage]).wait_send()
    whole(nb_send, nb_send_sem, nb_sem).wait_send()
    whole(own_recv.at[pl.ds(1, 2 * nx - 1)], own_send_sem, own_sem).wait_send()
    whole(k_recv.at[pl.ds(1, 2 * nx - 1)], k_send_sem, k_sem).wait_send()
    whole(x_recv.at[pl.ds(1, nx - 1)], x_send_sem, x_sem).wait_send()
    for n, (ref, count) in enumerate(((s_y, 2 * ny), (s_z, nz), (s_x, nx))):
        whole(ref.at[pl.ds(1, count - 1)], s_send_sem.at[n], s_sem.at[n]).wait_send()
    for turn in (0, 1):
        whole(a_recv.at[turn, pl.ds(1, 2 * nx - 1)], a_send_sem.at[turn], a_sem.at[turn]).wait_send()
        whole(b_recv.at[turn, pl.ds(1, ny - 1)], b_send_sem.at[turn], b_sem.at[turn]).wait_send()
        whole(c_recv.at[turn, pl.ds(1, nz - 1)], c_send_sem.at[turn], c_sem.at[turn]).wait_send()
        whole(d_recv.at[turn, pl.ds(1, 2 * nx - 1)], d_send_sem.at[turn], d_sem.at[turn]).wait_send()


def shards(
    sizes,
    jump_rhs,
    schur_blocks,
    dirichlet_blocks,
    block_columns,
    face_partner_slots,
    corner_basis,
    corner_owner,
    coarse_inverse,
):
    ny, nz, nx = sizes
    field = pltpu.VMEM((NB, LC, W), F32)
    far = pl.BlockSpec(memory_space=pl.ANY)
    near = pl.BlockSpec(memory_space=pltpu.VMEM)
    dma = pltpu.SemaphoreType.DMA
    dual, residual = pl.pallas_call(
        functools.partial(kernel, sizes),
        out_shape=(field, field),
        in_specs=[far] * 8,
        out_specs=(near, near),
        scratch_shapes=[
            pltpu.SMEM((KB, NB), jnp.int32),
            pltpu.SMEM((1, HALF), jnp.int32),
            pltpu.SMEM((1, NB), jnp.int32),
            pltpu.VMEM((NB, LC, W), F32),
            pltpu.VMEM((NB, KB, W, W), BF16),
            pltpu.VMEM((NB, KB, W, W), BF16),
            pltpu.VMEM((3, NB, W), F32),
            pltpu.VMEM((3 * W, 3 * W), F32),
            pltpu.SMEM((NB * KB,), jnp.int32),
            pltpu.VMEM((NB * KB, LC, W), F32),
            pltpu.VMEM((5, NB, LC, W), F32),
            pltpu.VMEM((5, 2, HALF, LC, W), F32),
            pltpu.VMEM((2, 16, W), F32),
            pltpu.VMEM((2, 16, W), F32),
            pltpu.VMEM((2, NB, W, W), BF16),
            pltpu.VMEM((2, 4, W), F32),
            pltpu.VMEM((2 * nx, 4, W), F32),
            pltpu.VMEM((3 * W, nx * W), BF16),
            pltpu.VMEM((2, 3 * W, 3 * W), BF16),
            pltpu.VMEM((2, 2, 4, W), F32),
            pltpu.VMEM((2, 2 * nx, 4, W), F32),
            pltpu.VMEM((2, ny, 2, 8, W), F32),
            pltpu.VMEM((2, nz, 2, 8, W), F32),
            pltpu.VMEM((2, nx, 4, W), F32),
            pltpu.VMEM((2, 2 * nx, 4, W), F32),
            pltpu.VMEM((4, NB, LC, W), F32),
            pltpu.VMEM((NB * KB, LIVE, W), F32),
            pltpu.VMEM((2, NB, W, W), BF16),
            pltpu.VMEM((2, LIVE, W), F32),
            pltpu.VMEM((2 * nx, LIVE, W), F32),
            pltpu.VMEM((2, nx, W, W), BF16),
            pltpu.VMEM((2 * nx, 4, W), F32),
            pltpu.VMEM((nx, nx, 4, W), F32),
            pltpu.VMEM((2 * ny, 8, W), F32),
            pltpu.VMEM((nz, 8, W), F32),
            pltpu.VMEM((nx, 8, W), F32),
            dma((8,)),
            dma((5,)),
            dma((5,)),
            dma(()),
            dma(()),
            dma(()),
            dma(()),
            dma((2,)),
            dma((2,)),
            dma((2,)),
            dma((2,)),
            dma((2,)),
            dma((2,)),
            dma((2,)),
            dma((2,)),
            dma(()),
            dma(()),
            dma(()),
            dma(()),
            dma((3,)),
            dma((3,)),
        ],
        compiler_params=pltpu.CompilerParams(
            collective_id=0, has_side_effects=True, vmem_limit_bytes=60 * 1024 * 1024
        ),
    )(
        block_columns[0, 0].T,
        face_partner_slots[0],
        corner_owner[0],
        jump_rhs[0, 0],
        schur_blocks[0, 0],
        dirichlet_blocks[0, 0],
        corner_basis[:, 0, 0],
        coarse_inverse[0],
    )
    return dual[None, None], residual[None, None]


def solution(mesh):
    sizes = plan(mesh.shape["sub"], mesh.shape["grp"])
    placed = (
        P("grp", "sub", None, None, None),
        P("grp", "sub", None, None, None, None),
        P("grp", "sub", None, None, None, None),
        P("grp", "sub", None, None),
        P("grp", "sub", None),
        P(None, "grp", "sub", None, None),
        P("grp", "sub", None),
        P("grp", None, None),
    )
    return jax.shard_map(
        functools.partial(shards, sizes),
        mesh=mesh,
        in_specs=placed,
        out_specs=(P("grp", "sub", None, None, None), P("grp", "sub", None, None, None)),
        check_vma=False,
    )
```

```python
import functools

import jax
import jax.numpy as jnp
from jax import lax
from jax.experimental import pallas as pl
from jax.experimental.pallas import tpu as pltpu
from jax.sharding import PartitionSpec as P

MESH = pl.DeviceIdType.MESH
F32 = jnp.float32
BF16 = jnp.bfloat16
W = 128
LC = 8
NB = 8
HALF = 4
KB = 4
NJ = 16
LIVE = 3 * NJ
LANE_ENERGY = 48


def plan(sub_count, grp_count):
    chips = sub_count // 2
    along_z = 1
    while along_z * along_z < chips:
        along_z *= 2
    return chips // along_z, along_z, grp_count


def far_first(count):
    return sorted(range(1, count), key=lambda t: -min(t, count - t))


def split(x):
    high = x.astype(BF16)
    low = (x - high.astype(F32)).astype(BF16)
    return high, low


def nn(a, b):
    return lax.dot_general(a, b, (((1,), (0,)), ((), ())), preferred_element_type=F32)


def nt(a, b):
    return lax.dot_general(a, b, (((1,), (1,)), ((), ())), preferred_element_type=F32)


def kernel(
    sizes,
    cols_hbm,
    match_hbm,
    owner_hbm,
    rhs_hbm,
    schur_hbm,
    dirichlet_hbm,
    basis_hbm,
    inverse_hbm,
    result,
    cols,
    match,
    owner,
    rhs,
    schur,
    dirichlet,
    basis,
    inverse,
    table,
    parts,
    faces,
    halo,
    nb_send,
    nb_recv,
    spread,
    onehot,
    inv_split,
    a_send,
    a_recv,
    b_recv,
    c_recv,
    d_send,
    d_recv,
    fields,
    kparts,
    moved,
    k_send,
    k_recv,
    k_pair,
    x_send,
    x_recv,
    s_y,
    s_z,
    s_x,
    load_sem,
    halo_send_sem,
    halo_sem,
    nb_send_sem,
    nb_sem,
    a_send_sem,
    a_sem,
    b_send_sem,
    b_sem,
    c_send_sem,
    c_sem,
    d_send_sem,
    d_sem,
    k_send_sem,
    k_sem,
    x_send_sem,
    x_sem,
    s_send_sem,
    s_sem,
):
    ny, nz, nx = sizes
    strips = ny * nz * 2
    k = lax.axis_index("sub")
    g = lax.axis_index("grp")
    core = lax.rem(k, 2)
    zi = lax.rem(k // 2, nz)
    yi = k // (2 * nz)

    def dev(sub, grp):
        return {"sub": sub, "grp": grp}

    up = dev(lax.rem(k + 1, strips), g)
    down = dev(lax.rem(k + strips - 1, strips), g)

    def line_x(step, other):
        sub = (k + 1 - 2 * core) if other else k
        return dev(sub, lax.rem(g + step, nx))

    def line_y(step):
        return dev((lax.rem(yi + step, ny) * nz + zi) * 2 + core, g)

    def line_z(step):
        return dev((yi * nz + lax.rem(zi + step, nz)) * 2 + core, g)

    x_peers = [(t, o) for t in far_first(nx) for o in (1, 0)] + [(0, 1)]

    barrier = pltpu.get_barrier_semaphore()
    lines = [(min(t, nx - t), line_x(t, o)) for t, o in x_peers]
    lines += [(min(t, ny - t), line_y(t)) for t in far_first(ny)]
    lines += [(min(t, nz - t), line_z(t)) for t in far_first(nz)]
    lines += [(2, up), (2, down)]
    greeted = [peer for _, peer in sorted(lines, key=lambda line: -line[0])]
    for peer in greeted:
        pl.semaphore_signal(barrier, inc=1, device_id=peer, device_id_type=MESH)

    loads = []
    for n, (source, target) in enumerate(
        (
            (rhs_hbm, rhs),
            (basis_hbm, basis),
            (dirichlet_hbm, dirichlet),
            (inverse_hbm, inverse),
            (schur_hbm, schur),
            (match_hbm, match),
            (cols_hbm, cols),
            (owner_hbm, owner),
        )
    ):
        copy = pltpu.make_async_copy(source, target, load_sem.at[n])
        loads.append(copy)
    for n in (5, 0, 6, 7, 1, 2, 4, 3):
        loads[n].start()

    for n in (5, 6, 7):
        loads[n].wait()
    at = [match[0, i] for i in range(HALF)]
    block_at = []
    for j in range(HALF):
        found = jnp.int32(0)
        for i in range(1, HALF):
            found = found + jnp.where(at[i] == j, jnp.int32(i), jnp.int32(0))
        block_at.append(found)
    block_at += [jnp.int32(b) for b in range(HALF, NB)]
    place_of = at + [jnp.int32(b) for b in range(HALF, NB)]

    for p in range(NB):
        b = block_at[p]
        table[p * KB] = b * KB
        for s in range(1, KB):
            c = cols[s, b]
            back = jnp.int32(0)
            for t in range(1, KB):
                back = back + jnp.where(cols[t, c] == b, jnp.int32(t), jnp.int32(0))
            table[p * KB + s] = c * KB + back

    loads[0].wait()
    for p in range(NB):
        faces[0, p] = rhs[block_at[p]]
    pl.semaphore_wait(barrier, len(greeted))

    def send_halo(stage):
        for side, peer in ((1, down), (0, up)):
            pltpu.make_async_remote_copy(
                src_ref=faces.at[stage, pl.ds(0 if side else HALF, HALF)],
                dst_ref=halo.at[stage, side],
                send_sem=halo_send_sem.at[stage],
                recv_sem=halo_sem.at[stage],
                device_id=peer,
                device_id_type=MESH,
            ).start()

    def whole(ref, send, recv):
        return pltpu.make_async_remote_copy(
            src_ref=ref, dst_ref=ref, send_sem=send, recv_sem=recv, device_id=up, device_id_type=MESH
        )

    def wait_halo(stage):
        whole(halo.at[stage], halo_send_sem.at[stage], halo_sem.at[stage]).wait_recv()

    def jump(stage):
        low = [faces[stage, p] - halo[stage, 0, p] for p in range(HALF)]
        high = [faces[stage, HALF + p] - halo[stage, 1, p] for p in range(HALF)]
        return low + high

    send_halo(0)

    lane = lax.broadcasted_iota(jnp.int32, (8, W), 1)
    loads[1].wait()
    owners = [owner[0, block_at[p]].astype(F32) for p in range(NB)]
    for side in (0, 1):
        nb_send[side] = jnp.zeros((16, W), F32)
        for c in range(3):
            for j in range(HALF):
                p = j if side else HALF + j
                nb_send[side, c * HALF + j] = basis[c, block_at[p]]
        tag = jnp.zeros((8, W), F32)
        for j in range(HALF):
            p = j if side else HALF + j
            spot = NB + j + (HALF if side else 0)
            tag = jnp.where(lane == LIVE + spot, owners[p], tag)
        nb_send[side, 12] = tag[0]
    for side, peer in ((1, down), (0, up)):
        pltpu.make_async_remote_copy(
            src_ref=nb_send.at[side],
            dst_ref=nb_recv.at[side],
            send_sem=nb_send_sem,
            recv_sem=nb_sem,
            device_id=peer,
            device_id_type=MESH,
        ).start()

    def block_product(matrix, source):
        for b in range(NB):
            high, low = split(fields[source, place_of[b]])
            row = jnp.concatenate([high, low], axis=0)
            product = nn(row, jnp.concatenate([matrix[b, s] for s in range(KB)], axis=1))
            product = product[:LC] + product[LC:]
            for s in range(KB):
                parts[b * KB + s] = product[:, s * W : (s + 1) * W]
        result = []
        for p in range(NB):
            total = parts[table[p * KB]]
            for s in range(1, KB):
                total = total + parts[table[p * KB + s]]
            result.append(total)
        return result

    def inner(first, second):
        total = first[0] * second[0]
        for u, v in zip(first[1:], second[1:]):
            total = total + u * v
        return jnp.sum(total, axis=1, keepdims=True)

    wait_halo(0)
    residual = jump(0)
    for p in range(NB):
        fields[0, p] = residual[p] + residual[p]
    loads[2].wait()
    lifted = block_product(dirichlet, 0)
    for p in range(NB):
        faces[1, p] = lifted[p]
    send_halo(1)
    rz0 = inner([fields[0, p] for p in range(NB)], lifted)

    whole(nb_recv, nb_send_sem, nb_sem).wait_recv()
    own_lanes = jnp.broadcast_to(nb_recv[0, pl.ds(12, 1)] + nb_recv[1, pl.ds(12, 1)], (8, W))
    for p in range(NB):
        own_lanes = jnp.where(lane == LIVE + p, owners[p], own_lanes)

    rows = []
    for c in range(3):
        rows += [basis[c, pl.ds(block_at[p], 1)] for p in range(HALF)]
        rows.append(basis[c, HALF:NB])
        rows.append(-nb_recv[0, c * HALF : (c + 1) * HALF])
        rows.append(-nb_recv[1, c * HALF : (c + 1) * HALF])
    rows = jnp.concatenate(rows + [jnp.zeros((W - LIVE, W), F32)], axis=0)
    row_place = lax.rem(lax.broadcasted_iota(jnp.int32, (W, W), 0), NB)
    for p in range(NB):
        high, low = split(jnp.where(row_place == p, rows, 0.0))
        spread[0, p] = high
        spread[1, p] = low

    def wide(ref, n):
        return jnp.concatenate([ref[n, p] for p in range(NB)], axis=1)

    def send_corner_sums(turn, lifted):
        doubled = jnp.concatenate([u + u for u in lifted], axis=1)
        high, low = split(doubled)
        first = nt(jnp.concatenate([high, low], axis=0), wide(spread, 0))
        sums = first[:LC] + first[LC:] + nt(high, wide(spread, 1))
        if turn == 0:
            sums = sums + own_lanes
        rolled = pltpu.roll(sums, 64, 1)
        mine = jnp.where(core == 0, sums[:4], sums[4:])
        a_send[turn, 0] = mine
        a_send[turn, 1] = jnp.where(core == 0, rolled[4:], rolled[:4])
        a_recv[turn, 0] = mine
        for t, o in x_peers:
            pltpu.make_async_remote_copy(
                src_ref=a_send.at[turn, o],
                dst_ref=a_recv.at[turn, 2 * t + o],
                send_sem=a_send_sem.at[turn],
                recv_sem=a_sem.at[turn],
                device_id=line_x(t, o),
                device_id_type=MESH,
            ).start()

    def pair(ref):
        high = ref.astype(BF16).astype(F32)
        return jnp.concatenate([high, ref - high], axis=0).astype(BF16)

    def assemble(turn):
        whole(a_recv.at[turn, pl.ds(1, 2 * nx - 1)], a_send_sem.at[turn], a_sem.at[turn]).wait_recv()
        tiles = [a_recv[turn, 2 * t] + a_recv[turn, 2 * t + 1] for t in range(nx)]
        if turn == 0:
            ids = jnp.concatenate([u[:1] for u in tiles], axis=0) - (g * W).astype(F32)
            corner = lax.broadcasted_iota(jnp.int32, (W, W), 0).astype(F32)
            mode = lax.rem(lax.broadcasted_iota(jnp.int32, (nx, W), 1), 64) // NJ
            for c in range(3):
                masked = jnp.where(mode == c, pltpu.roll(ids, W - LIVE + NJ * c, 1), -1.0)
                for t in range(nx):
                    onehot[c * W : (c + 1) * W, t * W : (t + 1) * W] = jnp.where(
                        corner == masked[t : t + 1], 1.0, 0.0
                    ).astype(BF16)
        else:
            whole(x_recv.at[pl.ds(1, nx - 1)], x_send_sem, x_sem).wait_recv()
            tiles = [u + x_send[t] for t, u in enumerate(tiles)]
            for d in range(1, nx):
                tiles = [u + x_recv[d, t] for t, u in enumerate(tiles)]
        came = jnp.concatenate(tiles, axis=1)
        dense = nt(pair(came), onehot[...])
        dense = dense[:4] + dense[4:]
        b_recv[turn, 0, 0] = jnp.concatenate([dense[:, :W], dense[:, W : 2 * W]], axis=0)
        b_recv[turn, 0, 1] = jnp.concatenate([dense[:, 2 * W :], jnp.zeros((4, W), F32)], axis=0)
        for t in far_first(ny):
            pltpu.make_async_remote_copy(
                src_ref=b_recv.at[turn, 0],
                dst_ref=b_recv.at[turn, t],
                send_sem=b_send_sem.at[turn],
                recv_sem=b_sem.at[turn],
                device_id=line_y(t),
                device_id_type=MESH,
            ).start()

    def total_of(ref, turn, count):
        sums = []
        for h in range(2):
            total = ref[turn, 0, h]
            for t in range(1, count):
                total = total + ref[turn, t, h]
            sums.append(total)
        return sums

    def across_z(turn):
        whole(b_recv.at[turn, pl.ds(1, ny - 1)], b_send_sem.at[turn], b_sem.at[turn]).wait_recv()
        for h, total in enumerate(total_of(b_recv, turn, ny)):
            c_recv[turn, 0, h] = total
        for t in far_first(nz):
            pltpu.make_async_remote_copy(
                src_ref=c_recv.at[turn, 0],
                dst_ref=c_recv.at[turn, t],
                send_sem=c_send_sem.at[turn],
                recv_sem=c_sem.at[turn],
                device_id=line_z(t),
                device_id_type=MESH,
            ).start()

    def solve(turn):
        whole(c_recv.at[turn, pl.ds(1, nz - 1)], c_send_sem.at[turn], c_sem.at[turn]).wait_recv()
        first, second = total_of(c_recv, turn, nz)
        summed = jnp.concatenate([first[:4], first[4:], second[:4]], axis=1)
        lhs = pair(summed)
        solved = nn(lhs, inv_split[0])
        solved = solved[:4] + solved[4:] + nn(lhs, inv_split[1])[:4]
        energy = jnp.sum(summed * solved, axis=1, keepdims=True) if turn else 0.0
        chosen = nn(pair(solved), onehot[...])
        chosen = chosen[:4] + chosen[4:]
        lane4 = lane[:4]
        for t in range(nx):
            d_send[turn, t] = jnp.where(lane4 == LANE_ENERGY, energy, chosen[:, t * W : (t + 1) * W])
        d_recv[turn, 0] = d_send[turn, 0]
        for t, o in x_peers:
            pltpu.make_async_remote_copy(
                src_ref=d_send.at[turn, t],
                dst_ref=d_recv.at[turn, 2 * t + o],
                send_sem=d_send_sem.at[turn],
                recv_sem=d_sem.at[turn],
                device_id=line_x(nx - t, o),
                device_id_type=MESH,
            ).start()
        return chosen

    def gathered(turn):
        whole(d_recv.at[turn, pl.ds(1, 2 * nx - 1)], d_send_sem.at[turn], d_sem.at[turn]).wait_recv()
        same, other = d_recv[turn, 0], d_recv[turn, 1]
        for t in range(1, nx):
            same = same + d_recv[turn, 2 * t]
            other = other + d_recv[turn, 2 * t + 1]
        both = jnp.where(
            core == 0, jnp.concatenate([same, other], axis=0), jnp.concatenate([other, same], axis=0)
        )
        turned = pltpu.roll(both, 64, 1)
        row_core = lax.broadcasted_iota(jnp.int32, (8, W), 0) // 4
        values = jnp.where(lane < LIVE, jnp.where(row_core == core, both, turned), 0.0)
        high, low = split(values)
        return high, low, both

    def expand(high, low, ref):
        mixed = nn(jnp.concatenate([high, low], axis=0), wide(ref, 0))
        mixed = mixed[:LC] + mixed[LC:] + nn(high, wide(ref, 1))
        return [mixed[:, p * W : (p + 1) * W] for p in range(NB)]

    send_corner_sums(0, lifted)

    for b in range(NB):
        p = place_of[b]
        row = jnp.concatenate([spread[0, p][:LIVE], spread[1, p][:LIVE]], axis=0)
        product = nn(row, jnp.concatenate([dirichlet[b, n] for n in range(KB)], axis=1))
        product = product[:LIVE] + product[LIVE:]
        for n in range(KB):
            kparts[b * KB + n] = product[:, n * W : (n + 1) * W]
    blank = jnp.zeros((W - LIVE, W), F32)
    for p in range(NB):
        total = kparts[table[p * KB]]
        for n in range(1, KB):
            total = total + kparts[table[p * KB + n]]
        high, low = split(jnp.concatenate([total, blank], axis=0))
        moved[0, p] = high
        moved[1, p] = low
    high, low = wide(moved, 0)[:LIVE], wide(moved, 1)[:LIVE]
    first = nt(jnp.concatenate([high, low], axis=0), wide(spread, 0))
    coupling = 4.0 * (first[:LIVE] + first[LIVE:] + nt(high, wide(spread, 1)))
    k_send[0] = coupling
    k_send[1] = pltpu.roll(coupling, 64, 1)
    k_recv[0] = coupling
    for t, o in x_peers:
        pltpu.make_async_remote_copy(
            src_ref=k_send.at[o],
            dst_ref=k_recv.at[2 * t + o],
            send_sem=k_send_sem,
            recv_sem=k_sem,
            device_id=line_x(t, o),
            device_id_type=MESH,
        ).start()

    def apply_schur(stage, source):
        wait_halo(stage - 1)
        for p, value in enumerate(jump(stage - 1)):
            fields[source, p] = value + value
        product = block_product(schur, source)
        for p in range(NB):
            faces[stage, p] = product[p]
        send_halo(stage)
        return product

    loads[4].wait()
    apply_schur(2, 1)
    assemble(0)

    wait_halo(2)
    for p, value in enumerate(jump(2)):
        fields[2, p] = value + value
    lifted = block_product(dirichlet, 2)
    for p in range(NB):
        faces[3, p] = lifted[p]
    send_corner_sums(1, lifted)
    loads[3].wait()
    high, low = split(inverse[...])
    inv_split[0] = high
    inv_split[1] = low
    across_z(0)
    whole(k_recv.at[pl.ds(1, 2 * nx - 1)], k_send_sem, k_sem).wait_recv()
    gap = jnp.zeros((64 - LIVE, W), F32)
    for t in range(nx):
        high, low = split(jnp.concatenate([k_recv[2 * t], gap, k_recv[2 * t + 1], gap], axis=0))
        k_pair[0, t] = high
        k_pair[1, t] = low

    chosen = pair(solve(0))
    for t in range(nx):
        tile = chosen[:, t * W : (t + 1) * W]
        both = nn(tile, k_pair[0, t])
        both = both[:4] + both[4:] + nn(tile, k_pair[1, t])[:4]
        x_send[t] = both
        x_send[nx + t] = both
    for d in far_first(nx):
        pltpu.make_async_remote_copy(
            src_ref=x_send.at[pl.ds(nx - d, nx)],
            dst_ref=x_recv.at[d],
            send_sem=x_send_sem,
            recv_sem=x_sem,
            device_id=line_x(d, 0),
            device_id_type=MESH,
        ).start()

    high, low, _ = gathered(0)
    for p, value in enumerate(expand(high, low, moved)):
        faces[3, p] = faces[3, p] + (value + value)
    send_halo(3)
    assemble(1)
    for p, value in enumerate(expand(high, low, spread)):
        fields[2, p] = fields[2, p] + (value + value)
    doubled = [fields[2, p] for p in range(NB)]
    g1 = inner([fields[1, p] for p in range(NB)], doubled) * 0.25
    m1 = inner(doubled, [faces[3, p] for p in range(NB)])

    product = apply_schur(4, 3)
    h1 = inner([fields[3, p] for p in range(NB)], product)
    scalars = jnp.zeros((8, W), F32)
    for n, value in enumerate((rz0, g1, m1, h1)):
        scalars = jnp.where(lane == n, value, scalars)

    def share(ref, step, peers, value):
        ref[0] = value
        for slot, peer in peers:
            pltpu.make_async_remote_copy(
                src_ref=ref.at[0],
                dst_ref=ref.at[slot],
                send_sem=s_send_sem.at[step],
                recv_sem=s_sem.at[step],
                device_id=peer,
                device_id_type=MESH,
            ).start()

    def shared(ref, step, count):
        whole(ref.at[pl.ds(1, count - 1)], s_send_sem.at[step], s_sem.at[step]).wait_recv()
        total = ref[0]
        for n in range(1, count):
            total = total + ref[n]
        return total

    share(s_y, 0, [(t, line_y(t)) for t in far_first(ny)], scalars)
    across_z(1)
    share(s_z, 1, [(t, line_z(t)) for t in far_first(nz)], shared(s_y, 0, ny))
    solve(1)
    share(s_x, 2, [(2 * t + o, line_x(t, o)) for t, o in x_peers], shared(s_z, 1, nz))
    high, low, both = gathered(1)
    mixed = expand(high, low, spread)
    sums = shared(s_x, 2, 2 * nx)

    def pick(n):
        return jnp.sum(jnp.where(lane == n, sums, 0.0), axis=1, keepdims=True)

    rz0, g1, m1, h1 = (pick(n) for n in range(4))
    h1 = h1 + jnp.sum(jnp.where(lane == LANE_ENERGY, both, 0.0), axis=1, keepdims=True)
    alpha0 = rz0 / g1
    rz1 = alpha0 * alpha0 * m1 - rz0
    grow = 1.0 + rz1 / rz0
    energy = grow * grow * g1 - 2.0 * grow * alpha0 * m1 + alpha0 * alpha0 * h1
    alpha1 = rz1 / energy
    first = alpha0 + alpha1 * grow
    second = -alpha1 * alpha0
    wait_halo(4)
    last = [u + v for u, v in zip(jump(4), mixed)]
    for p in range(NB):
        parts[p] = 0.5 * (first * fields[1, p] + second * fields[3, p])
        parts[NB + p] = 0.5 * (fields[0, p] - first * fields[2, p]) - second * last[p]
    for b in range(NB):
        result[0, b] = parts[place_of[b]]
        result[1, b] = parts[place_of[b] + NB]

    for stage in range(5):
        whole(halo.at[stage], halo_send_sem.at[stage], halo_sem.at[stage]).wait_send()
    whole(nb_send, nb_send_sem, nb_sem).wait_send()
    whole(k_recv.at[pl.ds(1, 2 * nx - 1)], k_send_sem, k_sem).wait_send()
    whole(x_recv.at[pl.ds(1, nx - 1)], x_send_sem, x_sem).wait_send()
    for n, (ref, count) in enumerate(((s_y, ny), (s_z, nz), (s_x, 2 * nx))):
        whole(ref.at[pl.ds(1, count - 1)], s_send_sem.at[n], s_sem.at[n]).wait_send()
    for turn in (0, 1):
        whole(a_recv.at[turn, pl.ds(1, 2 * nx - 1)], a_send_sem.at[turn], a_sem.at[turn]).wait_send()
        whole(b_recv.at[turn, pl.ds(1, ny - 1)], b_send_sem.at[turn], b_sem.at[turn]).wait_send()
        whole(c_recv.at[turn, pl.ds(1, nz - 1)], c_send_sem.at[turn], c_sem.at[turn]).wait_send()
        whole(d_recv.at[turn, pl.ds(1, 2 * nx - 1)], d_send_sem.at[turn], d_sem.at[turn]).wait_send()


def shards(
    sizes,
    jump_rhs,
    schur_blocks,
    dirichlet_blocks,
    block_columns,
    face_partner_slots,
    corner_basis,
    corner_owner,
    coarse_inverse,
):
    ny, nz, nx = sizes
    far = pl.BlockSpec(memory_space=pl.ANY)
    near = pl.BlockSpec(memory_space=pltpu.VMEM)
    dma = pltpu.SemaphoreType.DMA
    both = pl.pallas_call(
        functools.partial(kernel, sizes),
        out_shape=pltpu.VMEM((2, NB, LC, W), F32),
        in_specs=[far] * 8,
        out_specs=near,
        scratch_shapes=[
            pltpu.SMEM((KB, NB), jnp.int32),
            pltpu.SMEM((1, HALF), jnp.int32),
            pltpu.SMEM((1, NB), jnp.int32),
            pltpu.VMEM((NB, LC, W), F32),
            pltpu.VMEM((NB, KB, W, W), BF16),
            pltpu.VMEM((NB, KB, W, W), BF16),
            pltpu.VMEM((3, NB, W), F32),
            pltpu.VMEM((3 * W, 3 * W), F32),
            pltpu.SMEM((NB * KB,), jnp.int32),
            pltpu.VMEM((NB * KB, LC, W), F32),
            pltpu.VMEM((5, NB, LC, W), F32),
            pltpu.VMEM((5, 2, HALF, LC, W), F32),
            pltpu.VMEM((2, 16, W), F32),
            pltpu.VMEM((2, 16, W), F32),
            pltpu.VMEM((2, NB, W, W), BF16),
            pltpu.VMEM((3 * W, nx * W), BF16),
            pltpu.VMEM((2, 3 * W, 3 * W), BF16),
            pltpu.VMEM((2, 2, 4, W), F32),
            pltpu.VMEM((2, 2 * nx, 4, W), F32),
            pltpu.VMEM((2, ny, 2, 8, W), F32),
            pltpu.VMEM((2, nz, 2, 8, W), F32),
            pltpu.VMEM((2, nx, 4, W), F32),
            pltpu.VMEM((2, 2 * nx, 4, W), F32),
            pltpu.VMEM((4, NB, LC, W), F32),
            pltpu.VMEM((NB * KB, LIVE, W), F32),
            pltpu.VMEM((2, NB, W, W), BF16),
            pltpu.VMEM((2, LIVE, W), F32),
            pltpu.VMEM((2 * nx, LIVE, W), F32),
            pltpu.VMEM((2, nx, W, W), BF16),
            pltpu.VMEM((2 * nx, 4, W), F32),
            pltpu.VMEM((nx, nx, 4, W), F32),
            pltpu.VMEM((ny, 8, W), F32),
            pltpu.VMEM((nz, 8, W), F32),
            pltpu.VMEM((2 * nx, 8, W), F32),
            dma((8,)),
            dma((5,)),
            dma((5,)),
            dma(()),
            dma(()),
            dma((2,)),
            dma((2,)),
            dma((2,)),
            dma((2,)),
            dma((2,)),
            dma((2,)),
            dma((2,)),
            dma((2,)),
            dma(()),
            dma(()),
            dma(()),
            dma(()),
            dma((3,)),
            dma((3,)),
        ],
        compiler_params=pltpu.CompilerParams(
            collective_id=0, has_side_effects=True, vmem_limit_bytes=60 * 1024 * 1024
        ),
    )(
        block_columns[0, 0].T,
        face_partner_slots[0],
        corner_owner[0],
        jump_rhs[0, 0],
        schur_blocks[0, 0],
        dirichlet_blocks[0, 0],
        corner_basis[:, 0, 0],
        coarse_inverse[0],
    )
    return both[0][None, None], both[1][None, None]


def solution(mesh):
    sizes = plan(mesh.shape["sub"], mesh.shape["grp"])
    placed = (
        P("grp", "sub", None, None, None),
        P("grp", "sub", None, None, None, None),
        P("grp", "sub", None, None, None, None),
        P("grp", "sub", None, None),
        P("grp", "sub", None),
        P(None, "grp", "sub", None, None),
        P("grp", "sub", None),
        P("grp", None, None),
    )
    return jax.shard_map(
        functools.partial(shards, sizes),
        mesh=mesh,
        in_specs=placed,
        out_specs=(P("grp", "sub", None, None, None), P("grp", "sub", None, None, None)),
        check_vma=False,
    )
```

```python
import functools

import jax
import jax.numpy as jnp
from jax import lax
from jax.experimental import pallas as pl
from jax.experimental.pallas import tpu as pltpu
from jax.sharding import PartitionSpec as P

MESH = pl.DeviceIdType.MESH
F32 = jnp.float32
BF16 = jnp.bfloat16
W = 128
LC = 8
NB = 8
HALF = 4
KB = 4
NJ = 16
LIVE = 3 * NJ
LANE_ENERGY = 48


def plan(sub_count, grp_count):
    chips = sub_count // 2
    along_z = 1
    while along_z * along_z < chips:
        along_z *= 2
    return chips // along_z, along_z, grp_count


def far_first(count):
    return sorted(range(1, count), key=lambda t: -min(t, count - t))


def split(x):
    high = x.astype(BF16)
    low = (x - high.astype(F32)).astype(BF16)
    return high, low


def nn(a, b):
    return lax.dot_general(a, b, (((1,), (0,)), ((), ())), preferred_element_type=F32)


def nt(a, b):
    return lax.dot_general(a, b, (((1,), (1,)), ((), ())), preferred_element_type=F32)


def kernel(
    sizes,
    cols_hbm,
    match_hbm,
    owner_hbm,
    rhs_hbm,
    schur_hbm,
    dirichlet_hbm,
    basis_hbm,
    inverse_hbm,
    result,
    cols,
    match,
    owner,
    rhs,
    schur,
    dirichlet,
    basis,
    inverse,
    table,
    parts,
    faces,
    halo,
    nb_send,
    nb_recv,
    spread,
    onehot,
    inv_split,
    a_send,
    a_recv,
    b_recv,
    c_recv,
    d_send,
    d_recv,
    fields,
    kparts,
    moved,
    k_send,
    k_recv,
    k_pair,
    x_send,
    x_recv,
    s_y,
    s_z,
    s_x,
    load_sem,
    halo_send_sem,
    halo_sem,
    nb_send_sem,
    nb_sem,
    a_send_sem,
    a_sem,
    b_send_sem,
    b_sem,
    c_send_sem,
    c_sem,
    d_send_sem,
    d_sem,
    k_send_sem,
    k_sem,
    x_send_sem,
    x_sem,
    s_send_sem,
    s_sem,
):
    ny, nz, nx = sizes
    strips = ny * nz * 2
    k = lax.axis_index("sub")
    g = lax.axis_index("grp")
    core = lax.rem(k, 2)
    zi = lax.rem(k // 2, nz)
    yi = k // (2 * nz)

    def dev(sub, grp):
        return {"sub": sub, "grp": grp}

    up = dev(lax.rem(k + 1, strips), g)
    down = dev(lax.rem(k + strips - 1, strips), g)

    def line_x(step, other):
        sub = (k + 1 - 2 * core) if other else k
        return dev(sub, lax.rem(g + step, nx))

    def line_y(step):
        return dev((lax.rem(yi + step, ny) * nz + zi) * 2 + core, g)

    def line_z(step):
        return dev((yi * nz + lax.rem(zi + step, nz)) * 2 + core, g)

    x_peers = [(t, o) for t in far_first(nx) for o in (1, 0)] + [(0, 1)]

    barrier = pltpu.get_barrier_semaphore()
    lines = [(min(t, nx - t), line_x(t, o)) for t, o in x_peers]
    lines += [(min(t, ny - t), line_y(t)) for t in far_first(ny)]
    lines += [(min(t, nz - t), line_z(t)) for t in far_first(nz)]
    lines += [(2, up), (2, down)]
    greeted = [peer for _, peer in sorted(lines, key=lambda line: -line[0])]
    for peer in greeted:
        pl.semaphore_signal(barrier, inc=1, device_id=peer, device_id_type=MESH)

    loads = []
    for n, (source, target) in enumerate(
        (
            (rhs_hbm, rhs),
            (basis_hbm, basis),
            (dirichlet_hbm, dirichlet),
            (inverse_hbm, inverse),
            (schur_hbm, schur),
            (match_hbm, match),
            (cols_hbm, cols),
            (owner_hbm, owner),
        )
    ):
        copy = pltpu.make_async_copy(source, target, load_sem.at[n])
        loads.append(copy)
    for n in (5, 0, 6, 7, 1, 2, 4, 3):
        loads[n].start()

    for n in (5, 6, 7):
        loads[n].wait()
    at = [match[0, i] for i in range(HALF)]
    block_at = []
    for j in range(HALF):
        found = jnp.int32(0)
        for i in range(1, HALF):
            found = found + jnp.where(at[i] == j, jnp.int32(i), jnp.int32(0))
        block_at.append(found)
    block_at += [jnp.int32(b) for b in range(HALF, NB)]
    place_of = at + [jnp.int32(b) for b in range(HALF, NB)]

    for p in range(NB):
        b = block_at[p]
        table[p * KB] = b * KB
        for s in range(1, KB):
            c = cols[s, b]
            back = jnp.int32(0)
            for t in range(1, KB):
                back = back + jnp.where(cols[t, c] == b, jnp.int32(t), jnp.int32(0))
            table[p * KB + s] = c * KB + back

    loads[0].wait()
    for p in range(NB):
        faces[0, p] = rhs[block_at[p]]
    pl.semaphore_wait(barrier, len(greeted))

    def send_halo(stage):
        for side, peer in ((1, down), (0, up)):
            pltpu.make_async_remote_copy(
                src_ref=faces.at[stage, pl.ds(0 if side else HALF, HALF)],
                dst_ref=halo.at[stage, side],
                send_sem=halo_send_sem.at[stage],
                recv_sem=halo_sem.at[stage],
                device_id=peer,
                device_id_type=MESH,
            ).start()

    def whole(ref, send, recv):
        return pltpu.make_async_remote_copy(
            src_ref=ref, dst_ref=ref, send_sem=send, recv_sem=recv, device_id=up, device_id_type=MESH
        )

    def wait_halo(stage):
        whole(halo.at[stage], halo_send_sem.at[stage], halo_sem.at[stage]).wait_recv()

    def jump(stage):
        low = [faces[stage, p] - halo[stage, 0, p] for p in range(HALF)]
        high = [faces[stage, HALF + p] - halo[stage, 1, p] for p in range(HALF)]
        return low + high

    send_halo(0)

    lane = lax.broadcasted_iota(jnp.int32, (8, W), 1)
    loads[1].wait()
    owners = [owner[0, block_at[p]].astype(F32) for p in range(NB)]
    for side in (0, 1):
        nb_send[side] = jnp.zeros((16, W), F32)
        for c in range(3):
            for j in range(HALF):
                p = j if side else HALF + j
                nb_send[side, c * HALF + j] = basis[c, block_at[p]]
        tag = jnp.zeros((8, W), F32)
        for j in range(HALF):
            p = j if side else HALF + j
            spot = NB + j + (HALF if side else 0)
            tag = jnp.where(lane == LIVE + spot, owners[p], tag)
        nb_send[side, 12] = tag[0]
    for side, peer in ((1, down), (0, up)):
        pltpu.make_async_remote_copy(
            src_ref=nb_send.at[side],
            dst_ref=nb_recv.at[side],
            send_sem=nb_send_sem,
            recv_sem=nb_sem,
            device_id=peer,
            device_id_type=MESH,
        ).start()

    def block_product(matrix, source):
        for b in range(NB):
            high, low = split(fields[source, place_of[b]])
            row = jnp.concatenate([high, low], axis=0)
            product = nn(row, jnp.concatenate([matrix[b, s] for s in range(KB)], axis=1))
            product = product[:LC] + product[LC:]
            for s in range(KB):
                parts[b * KB + s] = product[:, s * W : (s + 1) * W]
        result = []
        for p in range(NB):
            total = parts[table[p * KB]]
            for s in range(1, KB):
                total = total + parts[table[p * KB + s]]
            result.append(total)
        return result

    def inner(first, second):
        total = first[0] * second[0]
        for u, v in zip(first[1:], second[1:]):
            total = total + u * v
        return jnp.sum(total, axis=1, keepdims=True)

    wait_halo(0)
    residual = jump(0)
    for p in range(NB):
        fields[0, p] = residual[p] + residual[p]
    loads[2].wait()
    lifted = block_product(dirichlet, 0)
    for p in range(NB):
        faces[1, p] = lifted[p]
    send_halo(1)
    rz0 = inner([fields[0, p] for p in range(NB)], lifted)

    whole(nb_recv, nb_send_sem, nb_sem).wait_recv()
    own_lanes = jnp.broadcast_to(nb_recv[0, pl.ds(12, 1)] + nb_recv[1, pl.ds(12, 1)], (8, W))
    for p in range(NB):
        own_lanes = jnp.where(lane == LIVE + p, owners[p], own_lanes)

    rows = []
    for c in range(3):
        rows += [basis[c, pl.ds(block_at[p], 1)] for p in range(HALF)]
        rows.append(basis[c, HALF:NB])
        rows.append(-nb_recv[0, c * HALF : (c + 1) * HALF])
        rows.append(-nb_recv[1, c * HALF : (c + 1) * HALF])
    rows = jnp.concatenate(rows + [jnp.zeros((W - LIVE, W), F32)], axis=0)
    row_place = lax.rem(lax.broadcasted_iota(jnp.int32, (W, W), 0), NB)
    for p in range(NB):
        high, low = split(jnp.where(row_place == p, rows, 0.0))
        spread[0, p] = high
        spread[1, p] = low

    def wide(ref, n):
        return jnp.concatenate([ref[n, p] for p in range(NB)], axis=1)

    def send_corner_sums(turn, lifted):
        doubled = jnp.concatenate([u + u for u in lifted], axis=1)
        high, low = split(doubled)
        first = nt(jnp.concatenate([high, low], axis=0), wide(spread, 0))
        sums = first[:LC] + first[LC:] + nt(high, wide(spread, 1))
        if turn == 0:
            sums = sums + own_lanes
        rolled = pltpu.roll(sums, 64, 1)
        mine = jnp.where(core == 0, sums[:4], sums[4:])
        a_send[turn, 0] = mine
        a_send[turn, 1] = jnp.where(core == 0, rolled[4:], rolled[:4])
        a_recv[turn, 0] = mine
        for t, o in x_peers:
            pltpu.make_async_remote_copy(
                src_ref=a_send.at[turn, o],
                dst_ref=a_recv.at[turn, 2 * t + o],
                send_sem=a_send_sem.at[turn],
                recv_sem=a_sem.at[turn],
                device_id=line_x(t, o),
                device_id_type=MESH,
            ).start()

    def pair(ref):
        high = ref.astype(BF16).astype(F32)
        return jnp.concatenate([high, ref - high], axis=0).astype(BF16)

    def assemble(turn):
        whole(a_recv.at[turn, pl.ds(1, 2 * nx - 1)], a_send_sem.at[turn], a_sem.at[turn]).wait_recv()
        tiles = [a_recv[turn, 2 * t] + a_recv[turn, 2 * t + 1] for t in range(nx)]
        if turn == 0:
            ids = jnp.concatenate([u[:1] for u in tiles], axis=0) - (g * W).astype(F32)
            corner = lax.broadcasted_iota(jnp.int32, (W, W), 0).astype(F32)
            mode = lax.rem(lax.broadcasted_iota(jnp.int32, (nx, W), 1), 64) // NJ
            for c in range(3):
                masked = jnp.where(mode == c, pltpu.roll(ids, W - LIVE + NJ * c, 1), -1.0)
                for t in range(nx):
                    onehot[c * W : (c + 1) * W, t * W : (t + 1) * W] = jnp.where(
                        corner == masked[t : t + 1], 1.0, 0.0
                    ).astype(BF16)
        else:
            whole(x_recv.at[pl.ds(1, nx - 1)], x_send_sem, x_sem).wait_recv()
            tiles = [u + x_send[t] for t, u in enumerate(tiles)]
            for d in range(1, nx):
                tiles = [u + x_recv[d, t] for t, u in enumerate(tiles)]
        came = jnp.concatenate(tiles, axis=1)
        dense = nt(pair(came), onehot[...])
        dense = dense[:4] + dense[4:]
        b_recv[turn, 0, 0] = jnp.concatenate([dense[:, :W], dense[:, W : 2 * W]], axis=0)
        b_recv[turn, 0, 1] = jnp.concatenate([dense[:, 2 * W :], jnp.zeros((4, W), F32)], axis=0)
        for t in far_first(ny):
            pltpu.make_async_remote_copy(
                src_ref=b_recv.at[turn, 0],
                dst_ref=b_recv.at[turn, t],
                send_sem=b_send_sem.at[turn],
                recv_sem=b_sem.at[turn],
                device_id=line_y(t),
                device_id_type=MESH,
            ).start()

    def total_of(ref, turn, count):
        sums = []
        for h in range(2):
            total = ref[turn, 0, h]
            for t in range(1, count):
                total = total + ref[turn, t, h]
            sums.append(total)
        return sums

    def across_z(turn):
        whole(b_recv.at[turn, pl.ds(1, ny - 1)], b_send_sem.at[turn], b_sem.at[turn]).wait_recv()
        for h, total in enumerate(total_of(b_recv, turn, ny)):
            c_recv[turn, 0, h] = total
        for t in far_first(nz):
            pltpu.make_async_remote_copy(
                src_ref=c_recv.at[turn, 0],
                dst_ref=c_recv.at[turn, t],
                send_sem=c_send_sem.at[turn],
                recv_sem=c_sem.at[turn],
                device_id=line_z(t),
                device_id_type=MESH,
            ).start()

    def solve(turn):
        whole(c_recv.at[turn, pl.ds(1, nz - 1)], c_send_sem.at[turn], c_sem.at[turn]).wait_recv()
        first, second = total_of(c_recv, turn, nz)
        summed = jnp.concatenate([first[:4], first[4:], second[:4]], axis=1)
        lhs = pair(summed)
        solved = nn(lhs, inv_split[0])
        solved = solved[:4] + solved[4:] + nn(lhs, inv_split[1])[:4]
        energy = jnp.sum(summed * solved, axis=1, keepdims=True) if turn else 0.0
        chosen = nn(pair(solved), onehot[...])
        chosen = chosen[:4] + chosen[4:]
        lane4 = lane[:4]
        for t in range(nx):
            d_send[turn, t] = jnp.where(lane4 == LANE_ENERGY, energy, chosen[:, t * W : (t + 1) * W])
        d_recv[turn, 0] = d_send[turn, 0]
        for t, o in x_peers:
            pltpu.make_async_remote_copy(
                src_ref=d_send.at[turn, t],
                dst_ref=d_recv.at[turn, 2 * t + o],
                send_sem=d_send_sem.at[turn],
                recv_sem=d_sem.at[turn],
                device_id=line_x(nx - t, o),
                device_id_type=MESH,
            ).start()
        return chosen

    def gathered(turn):
        whole(d_recv.at[turn, pl.ds(1, 2 * nx - 1)], d_send_sem.at[turn], d_sem.at[turn]).wait_recv()
        same, other = d_recv[turn, 0], d_recv[turn, 1]
        for t in range(1, nx):
            same = same + d_recv[turn, 2 * t]
            other = other + d_recv[turn, 2 * t + 1]
        both = jnp.where(
            core == 0, jnp.concatenate([same, other], axis=0), jnp.concatenate([other, same], axis=0)
        )
        turned = pltpu.roll(both, 64, 1)
        row_core = lax.broadcasted_iota(jnp.int32, (8, W), 0) // 4
        values = jnp.where(lane < LIVE, jnp.where(row_core == core, both, turned), 0.0)
        high, low = split(values)
        return high, low, both

    def expand(high, low, ref):
        mixed = nn(jnp.concatenate([high, low], axis=0), wide(ref, 0))
        mixed = mixed[:LC] + mixed[LC:] + nn(high, wide(ref, 1))
        return [mixed[:, p * W : (p + 1) * W] for p in range(NB)]

    send_corner_sums(0, lifted)

    for b in range(NB):
        p = place_of[b]
        row = jnp.concatenate([spread[0, p][:LIVE], spread[1, p][:LIVE]], axis=0)
        product = nn(row, jnp.concatenate([dirichlet[b, n] for n in range(KB)], axis=1))
        product = product[:LIVE] + product[LIVE:]
        for n in range(KB):
            kparts[b * KB + n] = product[:, n * W : (n + 1) * W]
    blank = jnp.zeros((W - LIVE, W), F32)
    for p in range(NB):
        total = kparts[table[p * KB]]
        for n in range(1, KB):
            total = total + kparts[table[p * KB + n]]
        high, low = split(jnp.concatenate([total, blank], axis=0))
        moved[0, p] = high
        moved[1, p] = low
    high, low = wide(moved, 0)[:LIVE], wide(moved, 1)[:LIVE]
    first = nt(jnp.concatenate([high, low], axis=0), wide(spread, 0))
    coupling = 4.0 * (first[:LIVE] + first[LIVE:] + nt(high, wide(spread, 1)))
    packed = coupling[: LIVE // 2] + pltpu.roll(coupling[LIVE // 2 :], 64, 1)
    k_send[...] = packed
    k_recv[0] = packed
    def apply_schur(stage, source):
        wait_halo(stage - 1)
        for p, value in enumerate(jump(stage - 1)):
            fields[source, p] = value + value
        product = block_product(schur, source)
        for p in range(NB):
            faces[stage, p] = product[p]
        send_halo(stage)
        return product

    loads[4].wait()
    apply_schur(2, 1)
    assemble(0)
    for t, o in x_peers:
        pltpu.make_async_remote_copy(
            src_ref=k_send,
            dst_ref=k_recv.at[2 * t + o],
            send_sem=k_send_sem,
            recv_sem=k_sem,
            device_id=line_x(t, o),
            device_id_type=MESH,
        ).start()

    wait_halo(2)
    for p, value in enumerate(jump(2)):
        fields[2, p] = value + value
    lifted = block_product(dirichlet, 2)
    for p in range(NB):
        faces[3, p] = lifted[p]
    send_corner_sums(1, lifted)
    loads[3].wait()
    high, low = split(inverse[...])
    inv_split[0] = high
    inv_split[1] = low
    across_z(0)
    whole(k_recv.at[pl.ds(1, 2 * nx - 1)], k_send_sem, k_sem).wait_recv()
    gap = jnp.zeros((64 - LIVE, W), F32)
    near_lanes = lax.broadcasted_iota(jnp.int32, (LIVE // 2, W), 1) < 64
    for t in range(nx):
        same, other = k_recv[2 * t], k_recv[2 * t + 1]
        rows = [
            jnp.where(near_lanes, same, 0.0),
            jnp.where(near_lanes, pltpu.roll(same, 64, 1), 0.0),
            gap,
            jnp.where(near_lanes, 0.0, pltpu.roll(other, 64, 1)),
            jnp.where(near_lanes, 0.0, other),
            gap,
        ]
        high, low = split(jnp.concatenate(rows, axis=0))
        k_pair[0, t] = high
        k_pair[1, t] = low

    chosen = pair(solve(0))
    for t in range(nx):
        tile = chosen[:, t * W : (t + 1) * W]
        both = nn(tile, k_pair[0, t])
        both = both[:4] + both[4:] + nn(tile, k_pair[1, t])[:4]
        x_send[t] = both
        x_send[nx + t] = both
    for d in far_first(nx):
        pltpu.make_async_remote_copy(
            src_ref=x_send.at[pl.ds(nx - d, nx)],
            dst_ref=x_recv.at[d],
            send_sem=x_send_sem,
            recv_sem=x_sem,
            device_id=line_x(d, 0),
            device_id_type=MESH,
        ).start()

    high, low, _ = gathered(0)
    for p, value in enumerate(expand(high, low, moved)):
        faces[3, p] = faces[3, p] + (value + value)
    send_halo(3)
    assemble(1)
    for p, value in enumerate(expand(high, low, spread)):
        fields[2, p] = fields[2, p] + (value + value)
    doubled = [fields[2, p] for p in range(NB)]
    g1 = inner([fields[1, p] for p in range(NB)], doubled) * 0.25
    m1 = inner(doubled, [faces[3, p] for p in range(NB)])

    product = apply_schur(4, 3)
    h1 = inner([fields[3, p] for p in range(NB)], product)
    scalars = jnp.zeros((8, W), F32)
    for n, value in enumerate((rz0, g1, m1, h1)):
        scalars = jnp.where(lane == n, value, scalars)

    def share(ref, step, peers, value):
        ref[0] = value
        for slot, peer in peers:
            pltpu.make_async_remote_copy(
                src_ref=ref.at[0],
                dst_ref=ref.at[slot],
                send_sem=s_send_sem.at[step],
                recv_sem=s_sem.at[step],
                device_id=peer,
                device_id_type=MESH,
            ).start()

    def shared(ref, step, count):
        whole(ref.at[pl.ds(1, count - 1)], s_send_sem.at[step], s_sem.at[step]).wait_recv()
        total = ref[0]
        for n in range(1, count):
            total = total + ref[n]
        return total

    share(s_y, 0, [(t, line_y(t)) for t in far_first(ny)], scalars)
    across_z(1)
    share(s_z, 1, [(t, line_z(t)) for t in far_first(nz)], shared(s_y, 0, ny))
    solve(1)
    share(s_x, 2, [(2 * t + o, line_x(t, o)) for t, o in x_peers], shared(s_z, 1, nz))
    high, low, both = gathered(1)
    mixed = expand(high, low, spread)
    sums = shared(s_x, 2, 2 * nx)

    def pick(n):
        return jnp.sum(jnp.where(lane == n, sums, 0.0), axis=1, keepdims=True)

    rz0, g1, m1, h1 = (pick(n) for n in range(4))
    h1 = h1 + jnp.sum(jnp.where(lane == LANE_ENERGY, both, 0.0), axis=1, keepdims=True)
    alpha0 = rz0 / g1
    rz1 = alpha0 * alpha0 * m1 - rz0
    grow = 1.0 + rz1 / rz0
    energy = grow * grow * g1 - 2.0 * grow * alpha0 * m1 + alpha0 * alpha0 * h1
    alpha1 = rz1 / energy
    first = alpha0 + alpha1 * grow
    second = -alpha1 * alpha0
    wait_halo(4)
    last = [u + v for u, v in zip(jump(4), mixed)]
    for p in range(NB):
        parts[p] = 0.5 * (first * fields[1, p] + second * fields[3, p])
        parts[NB + p] = 0.5 * (fields[0, p] - first * fields[2, p]) - second * last[p]
    for b in range(NB):
        result[0, b] = parts[place_of[b]]
        result[1, b] = parts[place_of[b] + NB]

    for stage in range(5):
        whole(halo.at[stage], halo_send_sem.at[stage], halo_sem.at[stage]).wait_send()
    whole(nb_send, nb_send_sem, nb_sem).wait_send()
    whole(k_recv.at[pl.ds(1, 2 * nx - 1)], k_send_sem, k_sem).wait_send()
    whole(x_recv.at[pl.ds(1, nx - 1)], x_send_sem, x_sem).wait_send()
    for n, (ref, count) in enumerate(((s_y, ny), (s_z, nz), (s_x, 2 * nx))):
        whole(ref.at[pl.ds(1, count - 1)], s_send_sem.at[n], s_sem.at[n]).wait_send()
    for turn in (0, 1):
        whole(a_recv.at[turn, pl.ds(1, 2 * nx - 1)], a_send_sem.at[turn], a_sem.at[turn]).wait_send()
        whole(b_recv.at[turn, pl.ds(1, ny - 1)], b_send_sem.at[turn], b_sem.at[turn]).wait_send()
        whole(c_recv.at[turn, pl.ds(1, nz - 1)], c_send_sem.at[turn], c_sem.at[turn]).wait_send()
        whole(d_recv.at[turn, pl.ds(1, 2 * nx - 1)], d_send_sem.at[turn], d_sem.at[turn]).wait_send()


def shards(
    sizes,
    jump_rhs,
    schur_blocks,
    dirichlet_blocks,
    block_columns,
    face_partner_slots,
    corner_basis,
    corner_owner,
    coarse_inverse,
):
    ny, nz, nx = sizes
    far = pl.BlockSpec(memory_space=pl.ANY)
    near = pl.BlockSpec(memory_space=pltpu.VMEM)
    dma = pltpu.SemaphoreType.DMA
    both = pl.pallas_call(
        functools.partial(kernel, sizes),
        out_shape=pltpu.VMEM((2, NB, LC, W), F32),
        in_specs=[far] * 8,
        out_specs=near,
        scratch_shapes=[
            pltpu.SMEM((KB, NB), jnp.int32),
            pltpu.SMEM((1, HALF), jnp.int32),
            pltpu.SMEM((1, NB), jnp.int32),
            pltpu.VMEM((NB, LC, W), F32),
            pltpu.VMEM((NB, KB, W, W), BF16),
            pltpu.VMEM((NB, KB, W, W), BF16),
            pltpu.VMEM((3, NB, W), F32),
            pltpu.VMEM((3 * W, 3 * W), F32),
            pltpu.SMEM((NB * KB,), jnp.int32),
            pltpu.VMEM((NB * KB, LC, W), F32),
            pltpu.VMEM((5, NB, LC, W), F32),
            pltpu.VMEM((5, 2, HALF, LC, W), F32),
            pltpu.VMEM((2, 16, W), F32),
            pltpu.VMEM((2, 16, W), F32),
            pltpu.VMEM((2, NB, W, W), BF16),
            pltpu.VMEM((3 * W, nx * W), BF16),
            pltpu.VMEM((2, 3 * W, 3 * W), BF16),
            pltpu.VMEM((2, 2, 4, W), F32),
            pltpu.VMEM((2, 2 * nx, 4, W), F32),
            pltpu.VMEM((2, ny, 2, 8, W), F32),
            pltpu.VMEM((2, nz, 2, 8, W), F32),
            pltpu.VMEM((2, nx, 4, W), F32),
            pltpu.VMEM((2, 2 * nx, 4, W), F32),
            pltpu.VMEM((4, NB, LC, W), F32),
            pltpu.VMEM((NB * KB, LIVE, W), F32),
            pltpu.VMEM((2, NB, W, W), BF16),
            pltpu.VMEM((LIVE // 2, W), F32),
            pltpu.VMEM((2 * nx, LIVE // 2, W), F32),
            pltpu.VMEM((2, nx, W, W), BF16),
            pltpu.VMEM((2 * nx, 4, W), F32),
            pltpu.VMEM((nx, nx, 4, W), F32),
            pltpu.VMEM((ny, 8, W), F32),
            pltpu.VMEM((nz, 8, W), F32),
            pltpu.VMEM((2 * nx, 8, W), F32),
            dma((8,)),
            dma((5,)),
            dma((5,)),
            dma(()),
            dma(()),
            dma((2,)),
            dma((2,)),
            dma((2,)),
            dma((2,)),
            dma((2,)),
            dma((2,)),
            dma((2,)),
            dma((2,)),
            dma(()),
            dma(()),
            dma(()),
            dma(()),
            dma((3,)),
            dma((3,)),
        ],
        compiler_params=pltpu.CompilerParams(
            collective_id=0, has_side_effects=True, vmem_limit_bytes=60 * 1024 * 1024
        ),
    )(
        block_columns[0, 0].T,
        face_partner_slots[0],
        corner_owner[0],
        jump_rhs[0, 0],
        schur_blocks[0, 0],
        dirichlet_blocks[0, 0],
        corner_basis[:, 0, 0],
        coarse_inverse[0],
    )
    return both[0][None, None], both[1][None, None]


def solution(mesh):
    sizes = plan(mesh.shape["sub"], mesh.shape["grp"])
    placed = (
        P("grp", "sub", None, None, None),
        P("grp", "sub", None, None, None, None),
        P("grp", "sub", None, None, None, None),
        P("grp", "sub", None, None),
        P("grp", "sub", None),
        P(None, "grp", "sub", None, None),
        P("grp", "sub", None),
        P("grp", None, None),
    )
    return jax.shard_map(
        functools.partial(shards, sizes),
        mesh=mesh,
        in_specs=placed,
        out_specs=(P("grp", "sub", None, None, None), P("grp", "sub", None, None, None)),
        check_vma=False,
    )
```
